128 devices in a mesh: outer: 4 (over z_lo, core), inner: 32 (over y, z_hi, x).
Axes of the slice: x: 4, y: 4, z: 4 (z_hi: 2, z_lo: 2; z = z_hi * 2 + z_lo), core: 2. Of those that a mesh axis runs over, the one named last changes fastest.
Arguments:
- coefficients: float32 [2, 5, 5, 128, 4096], P(None, None, None, ('outer', 'inner')), may hold values from -2.5 to 2.5
- speed_amp: float32 [8], replicated, may hold values from -0.12 to 0.12
- speed_wave: float32 [2, 8], replicated, may hold values from -24 to 24
- speed_shift: float32 [8], replicated, may hold values from -3.140625 to 3.140625
Outputs:
- transformed: float32 [2, 5, 5, 524288], P(None, None, None, ('outer', 'inner'))
The draws below stay inside these ranges and needn't reach their ends.
All inputs are finite; a program needn't handle non-finite values.
Results may differ from the reference program's by a relative error of at most 0.003.
Values sent between devices are 32-bit elements; how exact they have to be, the bound alone decides.
No kernel may reach another device: no remote copies, remote signals or barrier semaphores. Data moves between devices by JAX's collectives and lax.ppermute only.
A program may use at most 192 MiB of HBM per device.

```python
import math
import jax
import jax.numpy as jnp
import numpy as np
from jax import lax

N = 16384
CHEB = 5
MODES = 8
TX = 32
TY = 128
SOURCES = 128
TARGETS = 4096
N_OUTER = 4
N_INNER = 32


def with_spikes(values, stream_key, source, target, shards_of, factor):
    def block_of(dim):
        return (jnp.arange(values.shape[dim]) // (values.shape[dim] // shards_of)).reshape((-1,) + (1,) * (values.ndim - 1 - dim))

    near = jax.random.permutation(stream_key, shards_of)[block_of(target)]
    second = (block_of(target) + shards_of // 2) % shards_of
    return jnp.where((block_of(source) == near) | (block_of(source) == second), factor * values, values)


def levels(key, extent, split, least, largest):
    factor_of = 1.0
    for axis_at, shards_of in split:
        draws = jax.random.uniform(jax.random.fold_in(jax.random.fold_in(key, 6), axis_at), (shards_of,), jnp.float32, least / len(split), largest / len(split))
        factor_of = factor_of * jnp.repeat(jnp.exp(draws), extent[axis_at] // shards_of).reshape((-1,) + (1,) * (len(extent) - 1 - axis_at))
    return factor_of


def noise(own_key, extent, scale, limit, cuts=(), kind=jnp.bfloat16):
    values = jax.random.normal(own_key, extent, jnp.float32) * scale
    if len(cuts) > 0:
        values = levels(own_key, extent, cuts, -0.22, 0.18) * values
    return jnp.clip(values, min=-limit, max=limit).astype(kind)


def heavy_noise(stream_key, dims, deviation, reach, cuts, heavy, held_as=jnp.bfloat16):
    array = deviation * jax.random.normal(stream_key, dims, jnp.float32)
    if cuts:
        array = array * levels(stream_key, dims, cuts, -0.22, 0.18)
    return jnp.clip(with_spikes(array, jax.random.fold_in(stream_key, 3), *heavy), -reach, reach).astype(held_as)


def setup_inputs(seed: int = 0) -> dict:
    key_list = jax.random.split(jax.random.key(seed), 5)
    coefficients = heavy_noise(key_list[0], (2, CHEB, CHEB, SOURCES, TARGETS), 0.1, 2.5, ((3, 128),), (3, 4, 128, 5.5), jnp.float32)
    speed_amp = noise(key_list[1], (MODES,), 0.02, 0.12, (), jnp.float32)
    speed_wave = noise(key_list[2], (2, MODES), 4.0, 24.0, (), jnp.float32)
    speed_shift = jnp.clip(jax.random.uniform(key_list[3], (MODES,), jnp.float32, -3.140625, 3.140625), -3.140625, 3.140625)
    return dict(coefficients=coefficients, speed_amp=speed_amp, speed_wave=speed_wave, speed_shift=speed_shift)


TWO_PI = 2.0 * math.pi

def split_first(level_idx, total_bits):
    return (total_bits - 1 - level_idx) % 2 == 0

def box_widths(level_idx, total_bits):
    splits_x = sum((1 for bit_pos in range(total_bits) if split_first(bit_pos, total_bits)))
    splits_y = total_bits - splits_x
    before_x = sum((1 for bit_pos in range(level_idx) if split_first(bit_pos, total_bits)))
    before_y = level_idx - before_x
    return (2.0 ** splits_x / N / 2.0 ** before_x, 2.0 ** splits_y / N / 2.0 ** before_y)

def cheb_tables():
    points = 0.5 * np.cos(np.arange(CHEB) * np.pi / (CHEB - 1))
    child_points = np.stack([(half_idx - 0.5) / 2.0 + points / 2.0 for half_idx in (0, 1)], axis=1)
    lagrange = np.ones((2, CHEB, CHEB))
    for half_idx in range(2):
        for row_idx in range(CHEB):
            for col_idx in range(CHEB):
                for other_idx in range(CHEB):
                    if other_idx != col_idx:
                        lagrange[half_idx, row_idx, col_idx] *= (child_points[row_idx, half_idx] - points[other_idx]) / (points[col_idx] - points[other_idx])
    return (jnp.asarray(points, jnp.float32), jnp.asarray(child_points, jnp.float32), jnp.asarray(lagrange, jnp.float32))

def speed_field(pos_x, pos_y, speed_params):
    speed_amp, speed_wave, speed_shift = speed_params
    summed = jnp.zeros_like(pos_x + pos_y, dtype=jnp.float32)
    for mode_idx in range(MODES):
        summed = summed + speed_amp[mode_idx] * jnp.sin(TWO_PI * (speed_wave[0, mode_idx] * pos_x + speed_wave[1, mode_idx] * pos_y) + speed_shift[mode_idx])
    return summed

def source_centre(source_ids, level_idx, total_bits):
    freq_x = jnp.zeros_like(jnp.asarray(source_ids), dtype=jnp.float32)
    freq_y = jnp.zeros_like(jnp.asarray(source_ids), dtype=jnp.float32)
    for bit_pos in range(level_idx, total_bits):
        bit_sign = (source_ids // 2 ** (bit_pos - level_idx) % 2).astype(jnp.float32) - 0.5
        bit_depth = (total_bits - 1 - bit_pos) // 2 + 1
        if split_first(bit_pos, total_bits):
            freq_x = freq_x + bit_sign * (N / 2.0 ** bit_depth)
        else:
            freq_y = freq_y + bit_sign * (N / 2.0 ** bit_depth)
    return (freq_x, freq_y)

def start_centres(total_bits):
    box_index = jnp.arange(TX * TY, dtype=jnp.int32)
    width_x, width_y = box_widths(0, total_bits)
    centre_x = ((box_index // TY).astype(jnp.float32) + 0.5) * width_x
    centre_y = ((box_index % TY).astype(jnp.float32) + 0.5) * width_y
    return (centre_x, centre_y)

def expand_centres(centre_x, centre_y, level_idx, total_bits):
    width_x, width_y = box_widths(level_idx, total_bits)
    offsets = jnp.asarray([-0.25, 0.25], jnp.float32)
    if split_first(level_idx, total_bits):
        new_x = centre_x[..., None] + offsets * width_x
        new_y = jnp.broadcast_to(centre_y[..., None], new_x.shape)
    else:
        new_y = centre_y[..., None] + offsets * width_y
        new_x = jnp.broadcast_to(centre_x[..., None], new_y.shape)
    shape_new = centre_x.shape[:-1] + (centre_x.shape[-1] * 2,)
    return (new_x.reshape(shape_new), new_y.reshape(shape_new))

def level_geometry(centre_x, centre_y, level_idx, total_bits, speed_params):
    points, child_points, lagrange = cheb_tables()
    width_x, width_y = box_widths(level_idx, total_bits)
    extra = (1,) * centre_x.ndim
    nodes_x = points.reshape((CHEB, 1) + extra)
    nodes_y = points.reshape((1, CHEB) + extra)
    off_x = width_x * nodes_x
    off_y = width_y * nodes_y
    speed_centre = speed_field(centre_x, centre_y, speed_params)
    speed_near = speed_field(centre_x + off_x, centre_y + off_y, speed_params) - speed_centre
    along_x = split_first(level_idx, total_bits)
    if along_x:
        child_x = width_x * child_points.reshape((CHEB, 1) + extra + (2,))
        child_y = off_y[..., None]
    else:
        child_x = off_x[..., None]
        child_y = width_y * child_points.reshape((1, CHEB) + extra + (2,))
    speed_child = speed_field(centre_x[..., None] + child_x, centre_y[..., None] + child_y, speed_params) - speed_centre[..., None]
    return (off_x, off_y, speed_near, child_x, child_y, speed_child, lagrange, along_x)

def branch_term(values, centre, geometry):
    freq_x, freq_y = centre
    off_x, off_y, speed_near, child_x, child_y, speed_child, lagrange, along_x = geometry
    freq_abs = jnp.sqrt(freq_x * freq_x + freq_y * freq_y)
    phase_in = TWO_PI * (off_x * freq_x + off_y * freq_y + speed_near * freq_abs)
    cos_in = jnp.cos(phase_in)
    sin_in = jnp.sin(phase_in)
    rotated = jnp.stack([values[0] * cos_in + values[1] * sin_in, values[1] * cos_in - values[0] * sin_in])
    if along_x:
        interpolated = jnp.einsum('hab,rbc...->rac...h', lagrange, rotated, precision=lax.Precision.HIGHEST)
    else:
        interpolated = jnp.einsum('hcb,rab...->rac...h', lagrange, rotated, precision=lax.Precision.HIGHEST)
    phase_out = TWO_PI * (child_x * freq_x[..., None] + child_y * freq_y[..., None] + speed_child * freq_abs[..., None])
    cos_out = jnp.cos(phase_out)
    sin_out = jnp.sin(phase_out)
    return jnp.stack([interpolated[0] * cos_out - interpolated[1] * sin_out, interpolated[0] * sin_out + interpolated[1] * cos_out])

def run_levels(current, centre_x, centre_y, first_level, last_level, first_source, total_bits, speed_params):
    for level_idx in range(first_level, last_level):
        geometry = level_geometry(centre_x, centre_y, level_idx, total_bits, speed_params)
        source_count = current.shape[3]
        paired = current.reshape(current.shape[:3] + (source_count // 2, 2) + current.shape[4:])
        extra = (1,) * (current.ndim - 4)
        source_ids = first_source // 2 ** level_idx + 2 * jnp.arange(source_count // 2, dtype=jnp.int32)
        left_x, left_y = source_centre(source_ids, level_idx, total_bits)
        right_x, right_y = source_centre(source_ids + 1, level_idx, total_bits)
        left = (left_x.reshape((-1,) + extra), left_y.reshape((-1,) + extra))
        right = (right_x.reshape((-1,) + extra), right_y.reshape((-1,) + extra))
        summed = branch_term(paired[:, :, :, :, 0], left, geometry) + branch_term(paired[:, :, :, :, 1], right, geometry)
        current = summed.reshape(summed.shape[:-2] + (-1,))
        centre_x, centre_y = expand_centres(centre_x, centre_y, level_idx, total_bits)
    return (current, centre_x, centre_y)

def reference(coefficients, speed_amp, speed_wave, speed_shift):
    total_bits = (N_OUTER * N_INNER).bit_length() - 1
    speed_params = (speed_amp, speed_wave, speed_shift)
    centre_x, centre_y = start_centres(total_bits)
    current, centre_x, centre_y = run_levels(coefficients, centre_x[None], centre_y[None], 0, total_bits, 0, total_bits, speed_params)
    return current.reshape(2, CHEB, CHEB, -1)
```

```python
import math

import jax
import jax.numpy as jnp
import numpy as np
from jax import lax
from jax.experimental import pallas as pl
from jax.experimental.pallas import tpu as pltpu
from jax.sharding import PartitionSpec as P

N = 16384
CHEB = 5
MODES = 8
TX = 32
TY = 128
BITS = 7
DEVICES = 128
LANES = 128
NODES = CHEB * CHEB
PLANES = 2 * NODES
LOW = TX * TY // DEVICES
HALF = LOW // 2
PACK = LANES // LOW
PACKED = -(-PLANES // PACK)
LANE_BIT = (0, 1, 2, 3, 4, 5, 6)
LEVEL_TABLE = 8 * NODES
TABLE = 25
FIRST_ROW = BITS * TABLE
OFFSET_ROW = FIRST_ROW + 1 + 2 * CHEB
TWO_PI = 2.0 * math.pi
ROUND = 1.5 * 2.0**23
AXES = ("outer", "inner")


def split_first(level):
    return (BITS - 1 - level) % 2 == 0


def box_widths(level):
    splits_x = sum(1 for bit in range(BITS) if split_first(bit))
    splits_y = BITS - splits_x
    before_x = sum(1 for bit in range(level) if split_first(bit))
    before_y = level - before_x
    return (2.0**splits_x / N / 2.0**before_x, 2.0**splits_y / N / 2.0**before_y)


def points_of():
    points = 0.5 * np.cos(np.arange(CHEB) * np.pi / (CHEB - 1))
    child = np.stack([(half - 0.5) / 2.0 + points / 2.0 for half in (0, 1)])
    return points, child


def lagrange_of(u):
    points, _ = points_of()
    row = np.ones(CHEB)
    for j in range(CHEB):
        for m in range(CHEB):
            if m != j:
                row[j] *= (u - points[m]) / (points[j] - points[m])
    return row


def source_centre(ids, level):
    freq_x = np.zeros(len(ids))
    freq_y = np.zeros(len(ids))
    for bit in range(level, BITS):
        sign = (ids >> bit) % 2 - 0.5
        depth = (BITS - 1 - bit) // 2 + 1
        if split_first(bit):
            freq_x = freq_x + sign * (N / 2.0**depth)
        else:
            freq_y = freq_y + sign * (N / 2.0**depth)
    return freq_x, freq_y


def lane_tables():
    points, child = points_of()
    lane = np.arange(LANES)
    bit_of = [(lane >> LANE_BIT[k]) % 2 for k in range(BITS)]
    rows = []
    for level in range(BITS):
        width = box_widths(level)[0 if split_first(level) else 1]
        parent_id = sum(bit_of[k] << k for k in range(level + 1, BITS)) + 0 * lane
        parent_x, parent_y = source_centre(parent_id, level + 1)
        parent = np.sqrt(parent_x**2 + parent_y**2)
        centres = [source_centre(parent_id + (c << level), level) for c in range(2)]
        move_x = np.zeros(LANES)
        move_y = (lane % 2) * (HALF * box_widths(0)[1])
        for k in range(level):
            wide_x, wide_y = box_widths(k)
            half = (bit_of[k + 1] - 0.5) / 2.0
            if split_first(k):
                move_x = move_x + half * wide_x
            else:
                move_y = move_y + half * wide_y
        for c in range(2):
            rows.append(np.sqrt(centres[c][0] ** 2 + centres[c][1] ** 2) - parent)
        rows += [parent, move_x, move_y]
        for c in range(2):
            own_d, parent_d = (
                (centres[c][0], parent_x) if split_first(level) else (centres[c][1], parent_y)
            )
            for half in range(2):
                for i in range(CHEB):
                    turn = width * child[half, i] * own_d - width * points[i] / 2.0 * parent_d
                    rows.append(turn - np.round(turn))
    source = sum(bit_of[k] << k for k in range(BITS))
    freq_x, freq_y = source_centre(source, 0)
    wide_x, wide_y = box_widths(0)
    rows.append(-np.sqrt(freq_x**2 + freq_y**2))
    for i in range(CHEB):
        turn = -wide_x * points[i] * freq_x
        rows.append(turn - np.round(turn))
    for j in range(CHEB):
        turn = -wide_y * points[j] * freq_y
        rows.append(turn - np.round(turn))
    off_x, off_y = offset_tables()
    for level in range(BITS + 1):
        rows += [off_x[level], off_y[level]]
    while len(rows) % 8:
        rows.append(np.zeros(LANES))
    return np.stack(rows).astype(np.float32)


def offset_tables():
    points, child = points_of()
    off_x = np.zeros((BITS + 1, LANES))
    off_y = np.zeros((BITS + 1, LANES))
    for level in range(BITS + 1):
        wide_x, wide_y = box_widths(level % BITS)
        for a in range(CHEB):
            for b in range(CHEB):
                p = a * CHEB + b
                if level == BITS:
                    off_x[level, p], off_y[level, p] = wide_x * points[a], wide_y * points[b]
                elif split_first(level):
                    off_x[level, p], off_y[level, p] = wide_x * child[0, a], wide_y * points[b]
                else:
                    off_x[level, p], off_y[level, p] = wide_x * points[b], wide_y * child[0, a]
    return off_x, off_y


def chebyshev_fit(function, odd, terms):
    grid = 0.5 * np.cos((np.arange(400) + 0.5) * np.pi / 400)
    powers = np.stack([grid ** (2 * k + (1 if odd else 0)) for k in range(terms)], axis=1)
    answer, *_ = np.linalg.lstsq(powers, function(TWO_PI * grid), rcond=None)
    return [float(v) for v in answer]


SIN_FIT = chebyshev_fit(np.sin, True, 7)
COS_FIT = chebyshev_fit(np.cos, False, 7)


def horner(fit, square):
    total = fit[-1]
    for value in fit[-2::-1]:
        total = total * square + value
    return total


def sin_cos(turns):
    turns = turns - ((turns + ROUND) - ROUND)
    square = turns * turns
    return turns * horner(SIN_FIT, square), horner(COS_FIT, square)


def swap(left, right, shift, low):
    first = jnp.where(low, left, pltpu.roll(right, shift, 1))
    second = jnp.where(low, pltpu.roll(left, LANES - shift, 1), right)
    return first, second


def in_hbm(value):
    return pltpu.with_memory_space_constraint(value, pltpu.HBM)


def pack_kernel(rows_hbm, out_ref, in_ref, sems):
    rows = DEVICES // PACK
    lane = lax.broadcasted_iota(jnp.int32, (rows, LANES), 1)
    low64 = lane < 2 * LOW
    low32 = lane % (2 * LOW) < LOW
    copies = []
    for m in range(PACKED):
        start = PACK * m * rows
        size = min(PACK * rows, PLANES * rows - start)
        copies.append(
            pltpu.make_async_copy(
                rows_hbm.at[pl.ds(start, size)], in_ref.at[pl.ds(start, size)], sems.at[m]
            )
        )
        copies[m].start()
    for m in range(PACKED):
        copies[m].wait()
        blocks = []
        for n in range(PACK):
            plane = min(PACK * m + n, PLANES - 1)
            blocks.append(in_ref[plane * rows : (plane + 1) * rows, :])
        blocks[0], blocks[2] = swap(blocks[0], blocks[2], 2 * LOW, low64)
        blocks[1], blocks[3] = swap(blocks[1], blocks[3], 2 * LOW, low64)
        blocks[0], blocks[1] = swap(blocks[0], blocks[1], LOW, low32)
        blocks[2], blocks[3] = swap(blocks[2], blocks[3], LOW, low32)
        for r in range(PACK):
            out_ref[pl.ds(r * PACKED + m, rows, stride=PACK * PACKED), :] = blocks[r]


def pack(rows_in):
    return pl.pallas_call(
        pack_kernel,
        in_specs=[pl.BlockSpec(memory_space=pltpu.HBM)],
        out_specs=pl.BlockSpec(memory_space=pltpu.VMEM),
        out_shape=jax.ShapeDtypeStruct((DEVICES * PACKED, LANES), jnp.float32),
        scratch_shapes=[
            pltpu.VMEM((PLANES * DEVICES // PACK, LANES), jnp.float32),
            pltpu.SemaphoreType.DMA((PACKED,)),
        ],
        compiler_params=pltpu.CompilerParams(vmem_limit_bytes=16 * 2**20),
        cost_estimate=pl.CostEstimate(flops=10**6, bytes_accessed=1700000, transcendentals=0),
    )(in_hbm(rows_in))


def phase_kernel(
    amp_hbm,
    speed_hbm,
    shift_hbm,
    lane_hbm,
    table_hbm,
    first_hbm,
    amp_ref,
    speed_ref,
    shift_ref,
    lane_ref,
    table_ref,
    first_ref,
    row_ref,
    wave_ref,
    mode_ref,
    mode_smem,
    sems,
    out_sems,
):
    fetches = [
        pltpu.make_async_copy(source, target, sems.at[k])
        for k, (source, target) in enumerate(
            (
                (amp_hbm, amp_ref),
                (speed_hbm, speed_ref),
                (shift_hbm, shift_ref),
                (lane_hbm, lane_ref),
            )
        )
    ]
    for fetch in fetches:
        fetch.start()
    for fetch in fetches:
        fetch.wait()
    device = lax.axis_index(AXES)
    wide_x, wide_y = box_widths(0)
    per_row = TY // LOW
    base_x = (device // per_row).astype(jnp.float32) * wide_x + 0.5 * wide_x
    base_y = (device % per_row).astype(jnp.float32) * (LOW * wide_y) + 0.5 * wide_y

    which = lax.broadcasted_iota(jnp.int32, (MODES, LANES), 0)
    kx = jnp.zeros((MODES, LANES), jnp.float32)
    ky = jnp.zeros((MODES, LANES), jnp.float32)
    for mode in range(MODES):
        kx = jnp.where(which == mode, speed_ref[0, mode], kx)
        ky = jnp.where(which == mode, speed_ref[1, mode], ky)
    for level in range(BITS + 1):
        at = OFFSET_ROW + 2 * level
        turns = kx * lane_ref[at : at + 1, :] + ky * lane_ref[at + 1 : at + 2, :]
        half = 0.5 * turns
        half = half * horner(SIN_FIT, half * half)
        at = level * 2 * MODES
        mode_ref[at : at + MODES, :] = -2.0 * half * half
        mode_ref[at + MODES : at + 2 * MODES, :] = turns * horner(SIN_FIT, turns * turns)
    copy = pltpu.make_async_copy(mode_ref, mode_smem, sems.at[4])
    copy.start()

    low = lax.broadcasted_iota(jnp.int32, (LOW, LANES), 0).astype(jnp.float32) * wide_y
    for mode in range(MODES):
        at_base = (
            speed_ref[0, mode] * base_x
            + speed_ref[1, mode] * base_y
            + shift_ref[mode] * (1.0 / TWO_PI)
        )
        sine, cosine = sin_cos(at_base + speed_ref[1, mode] * low)
        row_ref[mode] = amp_ref[mode] * sine
        row_ref[MODES + mode] = amp_ref[mode] * cosine
    copy.wait()

    def differences(source_ref, level, p, groups):
        even = [None] * groups
        odd = [None] * groups
        for mode in range(MODES):
            less = mode_smem[level * 2 * MODES + mode, p]
            sine = mode_smem[level * 2 * MODES + MODES + mode, p]
            for t in range(groups):
                rows = slice(8 * t, 8 * t + 8)
                x = source_ref[mode, rows, :] * less
                y = source_ref[MODES + mode, rows, :] * sine
                even[t] = x if mode == 0 else even[t] + x
                odd[t] = y if mode == 0 else odd[t] + y
        return [(even[t] + odd[t], even[t] - odd[t]) for t in range(groups)]

    def put(ref, at, rows, turns):
        sine, cosine = sin_cos(turns)
        ref[at, rows, :] = cosine
        ref[at + 1, rows, :] = sine

    length = lane_ref[FIRST_ROW : FIRST_ROW + 1, :]

    def first_step(p, carry):
        a = p // CHEB
        b = p - a * CHEB
        line = (
            lane_ref[pl.ds(FIRST_ROW + 1 + a, 1), :]
            + lane_ref[pl.ds(FIRST_ROW + 1 + CHEB + b, 1), :]
        )
        back = (
            lane_ref[pl.ds(FIRST_ROW + CHEB - a, 1), :]
            + lane_ref[pl.ds(FIRST_ROW + 2 * CHEB - b, 1), :]
        )
        for t, (here, there) in enumerate(differences(row_ref, BITS, p, LOW // 8)):
            rows = slice(8 * t, 8 * t + 8)
            put(first_ref, 2 * p, rows, here * length + line)
            put(first_ref, 2 * (NODES - 1 - p), rows, there * length + back)
        return carry

    lax.fori_loop(0, NODES // 2 + 1, first_step, 0)
    first_copy = pltpu.make_async_copy(first_ref, first_hbm, sems.at[5])
    first_copy.start()

    def table_copy(level):
        part = pl.ds(level * LEVEL_TABLE, LEVEL_TABLE)
        return pltpu.make_async_copy(
            table_ref.at[part], table_hbm.at[part], out_sems.at[level]
        )

    def level_step(level, carry):
        top = level * TABLE
        apart = [lane_ref[pl.ds(top + c, 1), :] for c in range(2)]
        parent = lane_ref[pl.ds(top + 2, 1), :]
        move_x = lane_ref[pl.ds(top + 3, 1), :]
        move_y = lane_ref[pl.ds(top + 4, 1), :]
        for mode in range(MODES):
            sine, cosine = sin_cos(speed_ref[0, mode] * move_x + speed_ref[1, mode] * move_y)
            old_sine = row_ref[mode, :HALF, :]
            old_cosine = row_ref[MODES + mode, :HALF, :]
            wave_ref[mode] = old_sine * cosine + old_cosine * sine
            wave_ref[MODES + mode] = old_cosine * cosine - old_sine * sine
        moved = [
            (here * parent, there * parent)
            for here, there in differences(wave_ref, level, NODES // 2, HALF // 8)
        ]

        def pair_step(p, inner_carry):
            a = p // CHEB
            far = differences(wave_ref, level, p, HALF // 8)
            for c in range(2):
                line = lane_ref[pl.ds(top + 5 + 2 * CHEB * c + a, 1), :]
                back = lane_ref[pl.ds(top + 5 + 2 * CHEB * (c + 1) - 1 - a, 1), :]
                at = (2 * level + c) * (4 * NODES)
                for t in range(HALF // 8):
                    rows = slice(8 * t, 8 * t + 8)
                    put(table_ref, at + 2 * p, rows, far[t][0] * apart[c] + (moved[t][0] + line))
                    put(
                        table_ref,
                        at + 2 * (2 * NODES - 1 - p),
                        rows,
                        far[t][1] * apart[c] + (moved[t][1] + back),
                    )
            return inner_carry

        lax.fori_loop(0, NODES, pair_step, 0)
        table_copy(level).start()
        return carry

    lax.fori_loop(0, BITS, level_step, 0)
    first_copy.wait()
    for level in range(BITS):
        table_copy(level).wait()


def phases(speed_amp, speed_wave, speed_shift, lanes):
    return pl.pallas_call(
        phase_kernel,
        in_specs=[pl.BlockSpec(memory_space=pltpu.HBM)] * 4,
        out_specs=[pl.BlockSpec(memory_space=pltpu.HBM)] * 2,
        out_shape=[
            pltpu.HBM((BITS * LEVEL_TABLE, HALF, LANES), jnp.float32),
            pltpu.HBM((2 * NODES, LOW, LANES), jnp.float32),
        ],
        scratch_shapes=[
            pltpu.SMEM((MODES,), jnp.float32),
            pltpu.SMEM((2, MODES), jnp.float32),
            pltpu.SMEM((MODES,), jnp.float32),
            pltpu.VMEM(lanes.shape, jnp.float32),
            pltpu.VMEM((BITS * LEVEL_TABLE, HALF, LANES), jnp.float32),
            pltpu.VMEM((2 * NODES, LOW, LANES), jnp.float32),
            pltpu.VMEM((2 * MODES, LOW, LANES), jnp.float32),
            pltpu.VMEM((2 * MODES, HALF, LANES), jnp.float32),
            pltpu.VMEM(((BITS + 1) * 2 * MODES, LANES), jnp.float32),
            pltpu.SMEM(((BITS + 1) * 2 * MODES, LANES), jnp.float32),
            pltpu.SemaphoreType.DMA((6,)),
            pltpu.SemaphoreType.DMA((BITS,)),
        ],
        compiler_params=pltpu.CompilerParams(vmem_limit_bytes=32 * 2**20),
        cost_estimate=pl.CostEstimate(
            flops=70 * 10**6, bytes_accessed=13 * 10**6, transcendentals=3 * 10**6
        ),
    )(*map(in_hbm, (speed_amp, speed_wave, speed_shift, lanes)))


def interpolate(values):
    _, child = points_of()
    even0, odd0 = values[0] + values[4], values[0] - values[4]
    even1, odd1 = values[1] + values[3], values[1] - values[3]
    first = [values[2], None, None, None, values[4]]
    second = [values[0], None, None, None, values[2]]
    for i in range(1, CHEB - 1):
        row = lagrange_of(child[0, i])
        even = (
            float((row[0] + row[4]) / 2) * even0
            + float((row[1] + row[3]) / 2) * even1
            + float(row[2]) * values[2]
        )
        odd = float((row[0] - row[4]) / 2) * odd0 + float((row[1] - row[3]) / 2) * odd1
        first[i] = even + odd
        second[CHEB - 1 - i] = even - odd
    return first, second


def level_kernel(
    got_ref, table_hbm, first_hbm, out_ref, state_ref, table_ref, first_ref, sems
):
    copies = [pltpu.make_async_copy(first_hbm, first_ref, sems.at[BITS])]
    for level in range(BITS):
        part = pl.ds(level * LEVEL_TABLE, LEVEL_TABLE)
        copies.append(
            pltpu.make_async_copy(table_hbm.at[part], table_ref.at[part], sems.at[level])
        )
    for copy in copies:
        copy.start()
    for m in range(PACKED):
        block = got_ref[pl.ds(m, DEVICES, stride=PACKED), :].T
        for n in range(PACK):
            if PACK * m + n < PLANES:
                at = (PACK * m + n) * LOW
                state_ref[at : at + LOW, :] = block[n * LOW : (n + 1) * LOW, :]
    lane = lax.broadcasted_iota(jnp.int32, (8, LANES), 1)
    order = lane % 2
    for bit in range(1, BITS):
        order = order + ((lane >> (BITS - bit)) % 2 << bit)

    def line(level, b, t, places):
        shift = 2 ** LANE_BIT[level]
        low = lane // shift % 2 == 0
        sides = [[], []]
        for at in places:
            pair = []
            for half in range(2):
                row = half * HALF + 8 * t
                re = state_ref[pl.ds(at * LOW + row, 8), :]
                im = state_ref[pl.ds((NODES + at) * LOW + row, 8), :]
                if level == 0:
                    rows = slice(row, row + 8)
                    cosine, sine = first_ref[2 * at, rows, :], first_ref[2 * at + 1, rows, :]
                    re, im = re * cosine - im * sine, re * sine + im * cosine
                pair.append((re, im))
            re = swap(pair[0][0], pair[1][0], shift, low)
            im = swap(pair[0][1], pair[1][1], shift, low)
            for c in range(2):
                sides[c].append((re[c], im[c]))
        rows = slice(8 * t, 8 * t + 8)
        near = [
            [interpolate([value[r] for value in sides[c]]) for r in range(2)] for c in range(2)
        ]
        for a, at in enumerate(places):
            totals = []
            for half in range(2):
                real = imag = None
                for c in range(2):
                    e = 2 * (((2 * level + c) * 2 + half) * NODES + a * CHEB + b)
                    cosine, sine = table_ref[e, rows, :], table_ref[e + 1, rows, :]
                    re, im = near[c][0][half][a], near[c][1][half][a]
                    new_re, new_im = re * cosine - im * sine, re * sine + im * cosine
                    real = new_re if c == 0 else real + new_re
                    imag = new_im if c == 0 else imag + new_im
                totals.append((real, imag))
            for r in range(2):
                first, second = totals[0][r], totals[1][r]
                if level == BITS - 1:
                    first, second = swap(first, second, 1, lane % 2 == 0)
                    for half, value in enumerate((first, second)):
                        at_row = (at * LOW + half * HALF + 8 * t) * 2 + r
                        out_ref[pl.ds(at_row, 8, stride=2), :] = jnp.take_along_axis(
                            value, order, axis=1
                        )
                    continue
                at_row = (r * NODES + at) * LOW + 8 * t
                state_ref[pl.ds(at_row, 8), :] = first
                state_ref[pl.ds(at_row + HALF, 8), :] = second

    copies[0].wait()
    for level in range(BITS):
        copies[1 + level].wait()

        def step(b, carry, level=level):
            places = [
                a * CHEB + b if split_first(level) else b * CHEB + a for a in range(CHEB)
            ]
            for t in range(HALF // 8):
                line(level, b, t, places)
            return carry

        lax.fori_loop(0, CHEB, step, 0)


def levels(got, table, first):
    return pl.pallas_call(
        level_kernel,
        in_specs=[
            pl.BlockSpec(memory_space=pltpu.VMEM),
            pl.BlockSpec(memory_space=pltpu.HBM),
            pl.BlockSpec(memory_space=pltpu.HBM),
        ],
        out_specs=pl.BlockSpec(memory_space=pltpu.VMEM),
        out_shape=jax.ShapeDtypeStruct((PLANES * LOW, LANES), jnp.float32),
        scratch_shapes=[
            pltpu.VMEM((PLANES * LOW, LANES), jnp.float32),
            pltpu.VMEM((BITS * LEVEL_TABLE, HALF, LANES), jnp.float32),
            pltpu.VMEM((2 * NODES, LOW, LANES), jnp.float32),
            pltpu.SemaphoreType.DMA((BITS + 1,)),
        ],
        compiler_params=pltpu.CompilerParams(vmem_limit_bytes=32 * 2**20),
        cost_estimate=pl.CostEstimate(
            flops=22 * 10**6, bytes_accessed=14 * 10**6, transcendentals=0
        ),
    )(got, in_hbm(table), in_hbm(first))


def on_device(coefficients, speed_amp, speed_wave, speed_shift):
    packed = pack(coefficients.reshape(PLANES * (DEVICES // PACK), LANES))
    sent = packed.reshape(DEVICES, 1, PACKED * LANES)
    got = lax.all_to_all(sent, AXES, 0, 0, tiled=True)
    got = got.reshape(DEVICES * PACKED, LANES)
    table, first = phases(speed_amp, speed_wave, speed_shift, jnp.asarray(lane_tables()))
    final = levels(got, table, first).reshape(CHEB, CHEB, LOW, 2, LANES)
    return final.transpose(3, 0, 1, 2, 4).reshape(2, CHEB, CHEB, LOW * LANES)


def solution(mesh):
    in_specs = (P(None, None, None, AXES, None), P(), P(), P())
    out_specs = P(None, None, None, AXES)
    return jax.shard_map(
        on_device, mesh=mesh, in_specs=in_specs, out_specs=out_specs, check_vma=False
    )
```

```python
import math

import jax
import jax.numpy as jnp
import numpy as np
from jax import lax
from jax.experimental import pallas as pl
from jax.experimental.pallas import tpu as pltpu
from jax.sharding import PartitionSpec as P

N = 16384
CHEB = 5
MODES = 8
TX = 32
TY = 128
BITS = 7
DEVICES = 128
LANES = 128
NODES = CHEB * CHEB
PLANES = 2 * NODES
LOW = TX * TY // DEVICES
HALF = LOW // 2
PACK = LANES // LOW
PACKED = -(-PLANES // PACK)
LANE_BIT = (0, 1, 2, 3, 4, 5, 6)
LEVEL_TABLE = 8 * NODES
TABLE = 25
FIRST_ROW = BITS * TABLE
OFFSET_ROW = FIRST_ROW + 1 + 2 * CHEB
TWO_PI = 2.0 * math.pi
ROUND = 1.5 * 2.0**23
AXES = ("outer", "inner")


def split_first(level):
    return (BITS - 1 - level) % 2 == 0


def box_widths(level):
    splits_x = sum(1 for bit in range(BITS) if split_first(bit))
    splits_y = BITS - splits_x
    before_x = sum(1 for bit in range(level) if split_first(bit))
    before_y = level - before_x
    return (2.0**splits_x / N / 2.0**before_x, 2.0**splits_y / N / 2.0**before_y)


def points_of():
    points = 0.5 * np.cos(np.arange(CHEB) * np.pi / (CHEB - 1))
    child = np.stack([(half - 0.5) / 2.0 + points / 2.0 for half in (0, 1)])
    return points, child


def lagrange_of(u):
    points, _ = points_of()
    row = np.ones(CHEB)
    for j in range(CHEB):
        for m in range(CHEB):
            if m != j:
                row[j] *= (u - points[m]) / (points[j] - points[m])
    return row


def source_centre(ids, level):
    freq_x = np.zeros(len(ids))
    freq_y = np.zeros(len(ids))
    for bit in range(level, BITS):
        sign = (ids >> bit) % 2 - 0.5
        depth = (BITS - 1 - bit) // 2 + 1
        if split_first(bit):
            freq_x = freq_x + sign * (N / 2.0**depth)
        else:
            freq_y = freq_y + sign * (N / 2.0**depth)
    return freq_x, freq_y


def lane_tables():
    points, child = points_of()
    lane = np.arange(LANES)
    bit_of = [(lane >> LANE_BIT[k]) % 2 for k in range(BITS)]
    rows = []
    for level in range(BITS):
        width = box_widths(level)[0 if split_first(level) else 1]
        parent_id = sum(bit_of[k] << k for k in range(level + 1, BITS)) + 0 * lane
        parent_x, parent_y = source_centre(parent_id, level + 1)
        parent = np.sqrt(parent_x**2 + parent_y**2)
        centres = [source_centre(parent_id + (c << level), level) for c in range(2)]
        move_x = np.zeros(LANES)
        move_y = (lane % 2) * (HALF * box_widths(0)[1])
        for k in range(level):
            wide_x, wide_y = box_widths(k)
            half = (bit_of[k + 1] - 0.5) / 2.0
            if split_first(k):
                move_x = move_x + half * wide_x
            else:
                move_y = move_y + half * wide_y
        for c in range(2):
            rows.append(np.sqrt(centres[c][0] ** 2 + centres[c][1] ** 2) - parent)
        rows += [parent, move_x, move_y]
        for c in range(2):
            own_d, parent_d = (
                (centres[c][0], parent_x) if split_first(level) else (centres[c][1], parent_y)
            )
            for half in range(2):
                for i in range(CHEB):
                    turn = width * child[half, i] * own_d - width * points[i] / 2.0 * parent_d
                    rows.append(turn - np.round(turn))
    source = sum(bit_of[k] << k for k in range(BITS))
    freq_x, freq_y = source_centre(source, 0)
    wide_x, wide_y = box_widths(0)
    rows.append(-np.sqrt(freq_x**2 + freq_y**2))
    for i in range(CHEB):
        turn = -wide_x * points[i] * freq_x
        rows.append(turn - np.round(turn))
    for j in range(CHEB):
        turn = -wide_y * points[j] * freq_y
        rows.append(turn - np.round(turn))
    off_x, off_y = offset_tables()
    for level in range(BITS + 1):
        rows += [off_x[level], off_y[level]]
    while len(rows) % 8:
        rows.append(np.zeros(LANES))
    return np.stack(rows).astype(np.float32)


def offset_tables():
    points, child = points_of()
    off_x = np.zeros((BITS + 1, LANES))
    off_y = np.zeros((BITS + 1, LANES))
    for level in range(BITS + 1):
        wide_x, wide_y = box_widths(level % BITS)
        for a in range(CHEB):
            for b in range(CHEB):
                p = a * CHEB + b
                if level == BITS:
                    off_x[level, p], off_y[level, p] = wide_x * points[a], wide_y * points[b]
                elif split_first(level):
                    off_x[level, p], off_y[level, p] = wide_x * child[0, a], wide_y * points[b]
                else:
                    off_x[level, p], off_y[level, p] = wide_x * points[b], wide_y * child[0, a]
    return off_x, off_y


def chebyshev_fit(function, odd, terms):
    grid = 0.5 * np.cos((np.arange(400) + 0.5) * np.pi / 400)
    powers = np.stack([grid ** (2 * k + (1 if odd else 0)) for k in range(terms)], axis=1)
    answer, *_ = np.linalg.lstsq(powers, function(math.pi * grid), rcond=None)
    return [float(v) for v in answer]


SIN_FIT = chebyshev_fit(np.sin, True, 4)
COS_FIT = chebyshev_fit(np.cos, False, 5)
SIN_FINE = chebyshev_fit(np.sin, True, 6)
COS_FINE = chebyshev_fit(np.cos, False, 6)


def horner(fit, square):
    total = fit[-1]
    for value in fit[-2::-1]:
        total = total * square + value
    return total


def sin_cos(turns, sin_fit=SIN_FIT, cos_fit=COS_FIT):
    turns = turns - ((turns + ROUND) - ROUND)
    square = turns * turns
    sine = turns * horner(sin_fit, square)
    twice = sine + sine
    return twice * horner(cos_fit, square), 1.0 - twice * sine


def sin_cos_fine(turns):
    return sin_cos(turns, SIN_FINE, COS_FINE)


def swap(left, right, shift, low):
    first = jnp.where(low, left, pltpu.roll(right, shift, 1))
    second = jnp.where(low, pltpu.roll(left, LANES - shift, 1), right)
    return first, second


def in_hbm(value):
    return pltpu.with_memory_space_constraint(value, pltpu.HBM)


def pack_kernel(planes_hbm, out_hbm, in_ref, out_ref, in_sems, out_sems):
    lane = lax.broadcasted_iota(jnp.int32, (8, LANES), 1)
    high = lane >= 2 * LOW
    odd = lane % (2 * LOW) >= LOW
    groups = planes_hbm.shape[1] // 8
    size = 8 * PACK * PACKED
    fetches, stores = [], []
    for g in range(groups):
        fetches.append(
            pltpu.make_async_copy(
                planes_hbm.at[:, pl.ds(8 * g, 8), :], in_ref.at[g], in_sems.at[g]
            )
        )
        part = pl.ds(g * size, size)
        stores.append(
            pltpu.make_async_copy(out_ref.at[part], out_hbm.at[part], out_sems.at[g])
        )
    for fetch in fetches:
        fetch.start()
    for g in range(groups):
        fetches[g].wait()
        for m in range(PACKED):
            blocks = [in_ref[g, min(PACK * m + n, PLANES - 1)] for n in range(PACK)]
            blocks = [
                pltpu.roll(block, n * LOW, 1) if n else block for n, block in enumerate(blocks)
            ]
            for r in range(PACK):
                part = [blocks[(k - r) % PACK] for k in range(PACK)]
                turned = jnp.where(
                    high,
                    jnp.where(odd, part[3], part[2]),
                    jnp.where(odd, part[1], part[0]),
                )
                out_ref[pl.ds(g * size + r * PACKED + m, 8, stride=PACK * PACKED), :] = turned
        stores[g].start()
    for store in stores:
        store.wait()


def pack(planes):
    groups = planes.shape[1] // 8
    return pl.pallas_call(
        pack_kernel,
        in_specs=[pl.BlockSpec(memory_space=pltpu.HBM)],
        out_specs=pl.BlockSpec(memory_space=pltpu.HBM),
        out_shape=pltpu.HBM((DEVICES * PACKED, LANES), jnp.float32),
        scratch_shapes=[
            pltpu.VMEM((groups, PLANES, 8, LANES), jnp.float32),
            pltpu.VMEM((DEVICES * PACKED, LANES), jnp.float32),
            pltpu.SemaphoreType.DMA((groups,)),
            pltpu.SemaphoreType.DMA((groups,)),
        ],
        compiler_params=pltpu.CompilerParams(vmem_limit_bytes=16 * 2**20),
        cost_estimate=pl.CostEstimate(flops=10**6, bytes_accessed=1700000, transcendentals=0),
    )(in_hbm(planes))


def tree_sum(terms):
    while len(terms) > 1:
        terms = [terms[k] + terms[k + 1] for k in range(0, len(terms), 2)]
    return terms[0]


def phase_kernel(
    amp_hbm,
    speed_hbm,
    shift_hbm,
    lane_hbm,
    table_hbm,
    first_hbm,
    amp_ref,
    speed_ref,
    shift_ref,
    lane_ref,
    table_ref,
    first_ref,
    row_ref,
    wave_ref,
    mode_ref,
    mode_smem,
    sems,
    out_sems,
):
    fetches = [
        pltpu.make_async_copy(source, target, sems.at[k])
        for k, (source, target) in enumerate(
            (
                (amp_hbm, amp_ref),
                (speed_hbm, speed_ref),
                (shift_hbm, shift_ref),
                (lane_hbm, lane_ref),
            )
        )
    ]
    for fetch in fetches:
        fetch.start()
    for fetch in fetches:
        fetch.wait()
    device = lax.axis_index(AXES)
    wide_x, wide_y = box_widths(0)
    per_row = TY // LOW
    base_x = (device // per_row).astype(jnp.float32) * wide_x + 0.5 * wide_x
    base_y = (device % per_row).astype(jnp.float32) * (LOW * wide_y) + 0.5 * wide_y

    which = lax.broadcasted_iota(jnp.int32, (MODES, LANES), 0)
    kx = jnp.zeros((MODES, LANES), jnp.float32)
    ky = jnp.zeros((MODES, LANES), jnp.float32)
    for mode in range(MODES):
        kx = jnp.where(which == mode, speed_ref[0, mode], kx)
        ky = jnp.where(which == mode, speed_ref[1, mode], ky)
    for level in range(BITS + 1):
        at = OFFSET_ROW + 2 * level
        turns = kx * lane_ref[at : at + 1, :] + ky * lane_ref[at + 1 : at + 2, :]
        sine, _ = sin_cos_fine(turns)
        half = turns * horner(SIN_FINE, turns * turns)
        at = level * 2 * MODES
        mode_ref[at : at + MODES, :] = -2.0 * half * half
        mode_ref[at + MODES : at + 2 * MODES, :] = sine
    copy = pltpu.make_async_copy(mode_ref, mode_smem, sems.at[4])
    copy.start()

    low = lax.broadcasted_iota(jnp.int32, (LOW, LANES), 0).astype(jnp.float32) * wide_y
    for mode in range(MODES):
        at_base = (
            speed_ref[0, mode] * base_x
            + speed_ref[1, mode] * base_y
            + shift_ref[mode] * (1.0 / TWO_PI)
        )
        sine, cosine = sin_cos_fine(at_base + speed_ref[1, mode] * low)
        row_ref[mode] = amp_ref[mode] * sine
        row_ref[MODES + mode] = amp_ref[mode] * cosine
    copy.wait()

    def differences(source_ref, level, p, groups):
        even = [[] for _ in range(groups)]
        odd = [[] for _ in range(groups)]
        for mode in range(MODES):
            less = mode_smem[level * 2 * MODES + mode, p]
            sine = mode_smem[level * 2 * MODES + MODES + mode, p]
            for t in range(groups):
                rows = slice(8 * t, 8 * t + 8)
                even[t].append(source_ref[mode, rows, :] * less)
                odd[t].append(source_ref[MODES + mode, rows, :] * sine)
        sums = []
        for t in range(groups):
            x, y = tree_sum(even[t]), tree_sum(odd[t])
            sums.append((x + y, x - y))
        return tuple(sums)

    def put(ref, at, rows, turns):
        sine, cosine = sin_cos(turns)
        ref[at, rows, :] = cosine
        ref[at + 1, rows, :] = sine

    length = lane_ref[FIRST_ROW : FIRST_ROW + 1, :]

    def first_step(p, carry):
        a = p // CHEB
        b = p - a * CHEB
        line = (
            lane_ref[pl.ds(FIRST_ROW + 1 + a, 1), :]
            + lane_ref[pl.ds(FIRST_ROW + 1 + CHEB + b, 1), :]
        )
        back = (
            lane_ref[pl.ds(FIRST_ROW + CHEB - a, 1), :]
            + lane_ref[pl.ds(FIRST_ROW + 2 * CHEB - b, 1), :]
        )
        for t, (here, there) in enumerate(differences(row_ref, BITS, p, LOW // 8)):
            rows = slice(8 * t, 8 * t + 8)
            put(first_ref, 2 * p, rows, here * length + line)
            put(first_ref, 2 * (NODES - 1 - p), rows, there * length + back)
        return carry

    lax.fori_loop(0, NODES // 2 + 1, first_step, 0)
    first_copy = pltpu.make_async_copy(first_ref, first_hbm, sems.at[5])
    first_copy.start()

    def table_copy(level):
        part = pl.ds(level * LEVEL_TABLE, LEVEL_TABLE)
        return pltpu.make_async_copy(
            table_ref.at[part], table_hbm.at[part], out_sems.at[level]
        )

    def level_step(level, carry):
        top = level * TABLE
        apart = [lane_ref[pl.ds(top + c, 1), :] for c in range(2)]
        parent = lane_ref[pl.ds(top + 2, 1), :]
        move_x = lane_ref[pl.ds(top + 3, 1), :]
        move_y = lane_ref[pl.ds(top + 4, 1), :]
        for mode in range(MODES):
            sine, cosine = sin_cos_fine(speed_ref[0, mode] * move_x + speed_ref[1, mode] * move_y)
            old_sine = row_ref[mode, :HALF, :]
            old_cosine = row_ref[MODES + mode, :HALF, :]
            wave_ref[mode] = old_sine * cosine + old_cosine * sine
            wave_ref[MODES + mode] = old_cosine * cosine - old_sine * sine
        moved = [
            (here * parent, there * parent)
            for here, there in differences(wave_ref, level, NODES // 2, HALF // 8)
        ]

        def row_step(a, inner_carry):
            lines = [
                (
                    lane_ref[pl.ds(top + 5 + 2 * CHEB * c + a, 1), :],
                    lane_ref[pl.ds(top + 5 + 2 * CHEB * (c + 1) - 1 - a, 1), :],
                )
                for c in range(2)
            ]
            for b in range(CHEB):
                p = a * CHEB + b
                far = differences(wave_ref, level, p, HALF // 8)
                for c in range(2):
                    at = (2 * level + c) * (4 * NODES)
                    for t in range(HALF // 8):
                        rows = slice(8 * t, 8 * t + 8)
                        for k, place in enumerate((2 * p, 2 * (2 * NODES - 1 - p))):
                            turns = far[t][k] * apart[c] + (moved[t][k] + lines[c][k])
                            put(table_ref, at + place, rows, turns)
            return inner_carry

        lax.fori_loop(0, CHEB, row_step, 0)
        table_copy(level).start()
        return carry

    lax.fori_loop(0, BITS, level_step, 0)
    first_copy.wait()
    for level in range(BITS):
        table_copy(level).wait()


def phases(speed_amp, speed_wave, speed_shift, lanes):
    return pl.pallas_call(
        phase_kernel,
        in_specs=[pl.BlockSpec(memory_space=pltpu.HBM)] * 4,
        out_specs=[pl.BlockSpec(memory_space=pltpu.HBM)] * 2,
        out_shape=[
            pltpu.HBM((BITS * LEVEL_TABLE, HALF, LANES), jnp.float32),
            pltpu.HBM((2 * NODES, LOW, LANES), jnp.float32),
        ],
        scratch_shapes=[
            pltpu.SMEM((MODES,), jnp.float32),
            pltpu.SMEM((2, MODES), jnp.float32),
            pltpu.SMEM((MODES,), jnp.float32),
            pltpu.VMEM(lanes.shape, jnp.float32),
            pltpu.VMEM((BITS * LEVEL_TABLE, HALF, LANES), jnp.float32),
            pltpu.VMEM((2 * NODES, LOW, LANES), jnp.float32),
            pltpu.VMEM((2 * MODES, LOW, LANES), jnp.float32),
            pltpu.VMEM((2 * MODES, HALF, LANES), jnp.float32),
            pltpu.VMEM(((BITS + 1) * 2 * MODES, LANES), jnp.float32),
            pltpu.SMEM(((BITS + 1) * 2 * MODES, LANES), jnp.float32),
            pltpu.SemaphoreType.DMA((6,)),
            pltpu.SemaphoreType.DMA((BITS,)),
        ],
        compiler_params=pltpu.CompilerParams(vmem_limit_bytes=32 * 2**20),
        cost_estimate=pl.CostEstimate(
            flops=70 * 10**6, bytes_accessed=13 * 10**6, transcendentals=3 * 10**6
        ),
    )(*map(in_hbm, (speed_amp, speed_wave, speed_shift, lanes)))


def level_kernel(
    got_ref,
    table_hbm,
    first_hbm,
    out_hbm,
    state_ref,
    other_ref,
    table_ref,
    first_ref,
    out_ref,
    slot0_ref,
    slot1_ref,
    sems,
    out_sems,
):
    copies = [pltpu.make_async_copy(first_hbm, first_ref, sems.at[BITS])]
    for level in range(BITS):
        part = pl.ds(level * LEVEL_TABLE, LEVEL_TABLE)
        copies.append(
            pltpu.make_async_copy(table_hbm.at[part], table_ref.at[part], sems.at[level])
        )
    for copy in copies:
        copy.start()
    turn = lax.axis_index(AXES) % PACK
    for m in range(PACKED):
        block = got_ref[pl.ds(m, DEVICES, stride=PACKED), :].T
        for n in range(PACK):
            plane = PACK * m + lax.rem(n + PACK - turn, PACK)
            state_ref[pl.ds(pl.multiple_of(plane * LOW, LOW), LOW), :] = block[
                n * LOW : (n + 1) * LOW, :
            ]
    lane = lax.broadcasted_iota(jnp.int32, (8, LANES), 1)
    order = lane % 2
    for bit in range(1, BITS):
        order = order + ((lane >> (BITS - bit)) % 2 << bit)

    def places_of(level, b):
        return [a * CHEB + b if split_first(level) else b * CHEB + a for a in range(CHEB)]

    slots = (slot0_ref, slot1_ref)
    states = (state_ref, other_ref)

    def fetch(level, b, t):
        shift = 2 ** LANE_BIT[level]
        low = lane // shift % 2 == 0
        for a, at in enumerate(places_of(level, b)):
            pair = []
            for half in range(2):
                row = half * HALF + 8 * t
                re = states[level % 2][pl.ds(at * LOW + row, 8), :]
                im = states[level % 2][pl.ds((NODES + at) * LOW + row, 8), :]
                if level == 0:
                    rows = slice(row, row + 8)
                    cosine, sine = first_ref[2 * at, rows, :], first_ref[2 * at + 1, rows, :]
                    re, im = re * cosine - im * sine, re * sine + im * cosine
                pair.append((re, im))
            for r in range(2):
                for c, value in enumerate(swap(pair[0][r], pair[1][r], shift, low)):
                    slots[t][(2 * a + r) * 2 + c] = value

    def split(level, b, t, values):
        rows = slice(8 * t, 8 * t + 8)
        places = places_of(level, b)

        def rotated(half, a, near):
            real = imag = None
            for c in range(2):
                e = 2 * (((2 * level + c) * 2 + half) * NODES + a * CHEB + b)
                cosine, sine = table_ref[e, rows, :], table_ref[e + 1, rows, :]
                re, im = near[0][c], near[1][c]
                new_re, new_im = re * cosine - im * sine, re * sine + im * cosine
                real = new_re if c == 0 else real + new_re
                imag = new_im if c == 0 else imag + new_im
            return real, imag

        def keep(a, totals):
            for r in range(2):
                first, second = totals[0][r], totals[1][r]
                if level == BITS - 1:
                    first, second = swap(first, second, 1, lane % 2 == 0)
                    for half, value in enumerate((first, second)):
                        at_row = (half * HALF + 8 * t) * 2 + r
                        out_ref[a, b, pl.ds(at_row, 8, stride=2), :] = jnp.take_along_axis(
                            value, order, axis=1
                        )
                    continue
                at_row = (r * NODES + places[a]) * LOW + 8 * t
                states[1 - level % 2][pl.ds(at_row, 8), :] = first
                states[1 - level % 2][pl.ds(at_row + HALF, 8), :] = second

        ends = [[[values[a][r][c] for c in range(2)] for r in range(2)] for a in (0, 2, 4)]
        keep(0, (rotated(0, 0, ends[1]), rotated(1, 0, ends[0])))
        keep(4, (rotated(0, 4, ends[2]), rotated(1, 4, ends[1])))
        parts = [
            [
                (
                    values[0][r][c] + values[4][r][c],
                    values[1][r][c] + values[3][r][c],
                    values[0][r][c] - values[4][r][c],
                    values[1][r][c] - values[3][r][c],
                    values[2][r][c],
                )
                for c in range(2)
            ]
            for r in range(2)
        ]
        _, child = points_of()
        held = {}
        for i in range(1, CHEB - 1):
            row = lagrange_of(child[0, i])
            sums, gaps = [[], []], [[], []]
            for r in range(2):
                for c in range(2):
                    even0, even1, odd0, odd1, middle = parts[r][c]
                    even = (
                        float((row[0] + row[4]) / 2) * even0
                        + float((row[1] + row[3]) / 2) * even1
                        + float(row[2]) * middle
                    )
                    odd = (
                        float((row[0] - row[4]) / 2) * odd0
                        + float((row[1] - row[3]) / 2) * odd1
                    )
                    sums[r].append(even + odd)
                    gaps[r].append(even - odd)
            held[0, i] = rotated(0, i, sums)
            held[1, CHEB - 1 - i] = rotated(1, CHEB - 1 - i, gaps)
            for a in range(1, CHEB - 1):
                if (0, a) in held and (1, a) in held:
                    keep(a, (held.pop((0, a)), held.pop((1, a))))

    def out_copy(b):
        return pltpu.make_async_copy(out_ref.at[:, b], out_hbm.at[:, b], out_sems.at[b])

    copies[0].wait()
    for level in range(BITS):
        copies[1 + level].wait()
        for t in range(HALF // 8):
            fetch(level, 0, t)

        def step(b, carry, level=level):
            for t in range(HALF // 8):
                values = [
                    [[slots[t][(2 * a + r) * 2 + c] for c in range(2)] for r in range(2)]
                    for a in range(CHEB)
                ]
                fetch(level, jnp.minimum(b + 1, CHEB - 1), t)
                split(level, b, t, values)
            if level == BITS - 1:
                out_copy(b).start()
            return carry

        lax.fori_loop(0, CHEB, step, 0)
    for b in range(CHEB):
        out_copy(b).wait()


def levels(got, table, first):
    return pl.pallas_call(
        level_kernel,
        in_specs=[
            pl.BlockSpec(memory_space=pltpu.VMEM),
            pl.BlockSpec(memory_space=pltpu.HBM),
            pl.BlockSpec(memory_space=pltpu.HBM),
        ],
        out_specs=pl.BlockSpec(memory_space=pltpu.HBM),
        out_shape=pltpu.HBM((CHEB, CHEB, 2 * LOW, LANES), jnp.float32),
        scratch_shapes=[
            pltpu.VMEM((PACK * PACKED * LOW, LANES), jnp.float32),
            pltpu.VMEM((PLANES * LOW, LANES), jnp.float32),
            pltpu.VMEM((BITS * LEVEL_TABLE, HALF, LANES), jnp.float32),
            pltpu.VMEM((2 * NODES, LOW, LANES), jnp.float32),
            pltpu.VMEM((CHEB, CHEB, 2 * LOW, LANES), jnp.float32),
            pltpu.VMEM((4 * CHEB, 8, LANES), jnp.float32),
            pltpu.VMEM((4 * CHEB, 8, LANES), jnp.float32),
            pltpu.SemaphoreType.DMA((BITS + 1,)),
            pltpu.SemaphoreType.DMA((CHEB,)),
        ],
        compiler_params=pltpu.CompilerParams(vmem_limit_bytes=32 * 2**20),
        cost_estimate=pl.CostEstimate(
            flops=22 * 10**6, bytes_accessed=14 * 10**6, transcendentals=0
        ),
    )(got, in_hbm(table), in_hbm(first))


def on_device(coefficients, speed_amp, speed_wave, speed_shift):
    packed = pack(coefficients.reshape(PLANES, DEVICES // PACK, LANES))
    sent = packed.reshape(DEVICES, 1, PACKED * LANES)
    got = lax.all_to_all(sent, AXES, 0, 0, tiled=True)
    got = got.reshape(DEVICES * PACKED, LANES)
    table, first = phases(speed_amp, speed_wave, speed_shift, jnp.asarray(lane_tables()))
    final = levels(got, table, first).reshape(CHEB, CHEB, LOW, 2, LANES)
    return final.transpose(3, 0, 1, 2, 4).reshape(2, CHEB, CHEB, LOW * LANES)


def solution(mesh):
    in_specs = (P(None, None, None, AXES, None), P(), P(), P())
    out_specs = P(None, None, None, AXES)
    return jax.shard_map(
        on_device, mesh=mesh, in_specs=in_specs, out_specs=out_specs, check_vma=False
    )
```

```python
import math

import jax
import jax.numpy as jnp
import numpy as np
from jax import lax
from jax.experimental import pallas as pl
from jax.experimental.pallas import tpu as pltpu
from jax.sharding import PartitionSpec as P

N = 16384
CHEB = 5
MODES = 8
TX = 32
TY = 128
BITS = 7
DEVICES = 128
LANES = 128
NODES = CHEB * CHEB
PLANES = 2 * NODES
LOW = TX * TY // DEVICES
HALF = LOW // 2
PACK = LANES // LOW
PACKED = -(-PLANES // PACK)
LANE_BIT = (0, 1, 2, 3, 4, 5, 6)
LEVEL_TABLE = 8 * NODES
TABLE = 25
FIRST_ROW = BITS * TABLE
OFFSET_ROW = FIRST_ROW + 1 + 2 * CHEB
TWO_PI = 2.0 * math.pi
ROUND = 1.5 * 2.0**23
AXES = ("outer", "inner")


def split_first(level):
    return (BITS - 1 - level) % 2 == 0


def box_widths(level):
    splits_x = sum(1 for bit in range(BITS) if split_first(bit))
    splits_y = BITS - splits_x
    before_x = sum(1 for bit in range(level) if split_first(bit))
    before_y = level - before_x
    return (2.0**splits_x / N / 2.0**before_x, 2.0**splits_y / N / 2.0**before_y)


def points_of():
    points = 0.5 * np.cos(np.arange(CHEB) * np.pi / (CHEB - 1))
    child = np.stack([(half - 0.5) / 2.0 + points / 2.0 for half in (0, 1)])
    return points, child


def lagrange_of(u):
    points, _ = points_of()
    row = np.ones(CHEB)
    for j in range(CHEB):
        for m in range(CHEB):
            if m != j:
                row[j] *= (u - points[m]) / (points[j] - points[m])
    return row


def source_centre(ids, level):
    freq_x = np.zeros(len(ids))
    freq_y = np.zeros(len(ids))
    for bit in range(level, BITS):
        sign = (ids >> bit) % 2 - 0.5
        depth = (BITS - 1 - bit) // 2 + 1
        if split_first(bit):
            freq_x = freq_x + sign * (N / 2.0**depth)
        else:
            freq_y = freq_y + sign * (N / 2.0**depth)
    return freq_x, freq_y


def lane_tables():
    points, child = points_of()
    lane = np.arange(LANES)
    bit_of = [(lane >> LANE_BIT[k]) % 2 for k in range(BITS)]
    rows = []
    for level in range(BITS):
        width = box_widths(level)[0 if split_first(level) else 1]
        parent_id = sum(bit_of[k] << k for k in range(level + 1, BITS)) + 0 * lane
        parent_x, parent_y = source_centre(parent_id, level + 1)
        parent = np.sqrt(parent_x**2 + parent_y**2)
        centres = [source_centre(parent_id + (c << level), level) for c in range(2)]
        move_x = np.zeros(LANES)
        move_y = (lane % 2) * (HALF * box_widths(0)[1])
        for k in range(level):
            wide_x, wide_y = box_widths(k)
            half = (bit_of[k + 1] - 0.5) / 2.0
            if split_first(k):
                move_x = move_x + half * wide_x
            else:
                move_y = move_y + half * wide_y
        for c in range(2):
            rows.append(np.sqrt(centres[c][0] ** 2 + centres[c][1] ** 2) - parent)
        rows += [parent, move_x, move_y]
        for c in range(2):
            own_d, parent_d = (
                (centres[c][0], parent_x) if split_first(level) else (centres[c][1], parent_y)
            )
            for half in range(2):
                for i in range(CHEB):
                    turn = width * child[half, i] * own_d - width * points[i] / 2.0 * parent_d
                    rows.append(turn - np.round(turn))
    source = sum(bit_of[k] << k for k in range(BITS))
    freq_x, freq_y = source_centre(source, 0)
    wide_x, wide_y = box_widths(0)
    rows.append(-np.sqrt(freq_x**2 + freq_y**2))
    for i in range(CHEB):
        turn = -wide_x * points[i] * freq_x
        rows.append(turn - np.round(turn))
    for j in range(CHEB):
        turn = -wide_y * points[j] * freq_y
        rows.append(turn - np.round(turn))
    off_x, off_y = offset_tables()
    for level in range(BITS + 1):
        rows += [off_x[level], off_y[level]]
    while len(rows) % 8:
        rows.append(np.zeros(LANES))
    return np.stack(rows).astype(np.float32)


def offset_tables():
    points, child = points_of()
    off_x = np.zeros((BITS + 1, LANES))
    off_y = np.zeros((BITS + 1, LANES))
    for level in range(BITS + 1):
        wide_x, wide_y = box_widths(level % BITS)
        for a in range(CHEB):
            for b in range(CHEB):
                p = a * CHEB + b
                if level == BITS:
                    off_x[level, p], off_y[level, p] = wide_x * points[a], wide_y * points[b]
                elif split_first(level):
                    off_x[level, p], off_y[level, p] = wide_x * child[0, a], wide_y * points[b]
                else:
                    off_x[level, p], off_y[level, p] = wide_x * points[b], wide_y * child[0, a]
    return off_x, off_y


def chebyshev_fit(function, odd, terms):
    grid = 0.5 * np.cos((np.arange(400) + 0.5) * np.pi / 400)
    powers = np.stack([grid ** (2 * k + (1 if odd else 0)) for k in range(terms)], axis=1)
    answer, *_ = np.linalg.lstsq(powers, function(math.pi * grid), rcond=None)
    return [float(v) for v in answer]


SIN_FIT = chebyshev_fit(np.sin, True, 4)
COS_FIT = chebyshev_fit(np.cos, False, 5)
SIN_FINE = chebyshev_fit(np.sin, True, 6)
COS_FINE = chebyshev_fit(np.cos, False, 6)


def horner(fit, square):
    total = fit[-1]
    for value in fit[-2::-1]:
        total = total * square + value
    return total


def sin_cos(turns, sin_fit=SIN_FIT, cos_fit=COS_FIT):
    turns = turns - ((turns + ROUND) - ROUND)
    square = turns * turns
    sine = turns * horner(sin_fit, square)
    twice = sine + sine
    return twice * horner(cos_fit, square), 1.0 - twice * sine


def sin_cos_fine(turns):
    return sin_cos(turns, SIN_FINE, COS_FINE)


def swap(left, right, shift, low):
    first = jnp.where(low, left, pltpu.roll(right, shift, 1))
    second = jnp.where(low, pltpu.roll(left, LANES - shift, 1), right)
    return first, second


def in_hbm(value):
    return pltpu.with_memory_space_constraint(value, pltpu.HBM)


def pack_kernel(planes_hbm, out_hbm, in_ref, out_ref, in_sems, out_sems):
    lane = lax.broadcasted_iota(jnp.int32, (8, LANES), 1)
    high = lane >= 2 * LOW
    odd = lane % (2 * LOW) >= LOW
    groups = planes_hbm.shape[1] // 8

    def fetch(g):
        rows = pl.ds(pl.multiple_of(8 * g, 8), 8)
        return pltpu.make_async_copy(planes_hbm.at[:, rows, :], in_ref.at[g], in_sems.at[g])

    def store(g):
        part = pl.ds(pl.multiple_of(g * size, 8), size)
        return pltpu.make_async_copy(out_ref.at[part], out_hbm.at[part], out_sems.at[g])

    def group_step(g, carry):
        fetch(g).wait()
        for m in range(PACKED):
            blocks = [in_ref[g, min(PACK * m + n, PLANES - 1)] for n in range(PACK)]
            blocks = [
                pltpu.roll(block, n * LOW, 1) if n else block for n, block in enumerate(blocks)
            ]
            for r in range(PACK):
                part = [blocks[(k - r) % PACK] for k in range(PACK)]
                turned = jnp.where(
                    high,
                    jnp.where(odd, part[3], part[2]),
                    jnp.where(odd, part[1], part[0]),
                )
                out_ref[pl.ds(g * size + r * PACKED + m, 8, stride=PACK * PACKED), :] = turned
        store(g).start()
        return carry

    size = 8 * PACK * PACKED
    for g in range(groups):
        fetch(g).start()
    lax.fori_loop(0, groups, group_step, 0)
    for g in range(groups):
        store(g).wait()


def pack(planes):
    groups = planes.shape[1] // 8
    return pl.pallas_call(
        pack_kernel,
        in_specs=[pl.BlockSpec(memory_space=pltpu.HBM)],
        out_specs=pl.BlockSpec(memory_space=pltpu.HBM),
        out_shape=pltpu.HBM((DEVICES * PACKED, LANES), jnp.float32),
        scratch_shapes=[
            pltpu.VMEM((groups, PLANES, 8, LANES), jnp.float32),
            pltpu.VMEM((DEVICES * PACKED, LANES), jnp.float32),
            pltpu.SemaphoreType.DMA((groups,)),
            pltpu.SemaphoreType.DMA((groups,)),
        ],
        compiler_params=pltpu.CompilerParams(vmem_limit_bytes=16 * 2**20),
        cost_estimate=pl.CostEstimate(flops=10**6, bytes_accessed=1700000, transcendentals=0),
    )(in_hbm(planes))


def tree_sum(terms):
    while len(terms) > 1:
        terms = [terms[k] + terms[k + 1] for k in range(0, len(terms), 2)]
    return terms[0]


def phase_kernel(
    amp_hbm,
    speed_hbm,
    shift_hbm,
    lane_hbm,
    table_hbm,
    table0_ref,
    first_ref,
    amp_ref,
    speed_ref,
    shift_ref,
    lane_ref,
    table_ref,
    row_ref,
    wave_ref,
    mode_ref,
    mode_smem,
    sems,
    out_sems,
):
    fetches = [
        pltpu.make_async_copy(source, target, sems.at[k])
        for k, (source, target) in enumerate(
            (
                (amp_hbm, amp_ref),
                (speed_hbm, speed_ref),
                (shift_hbm, shift_ref),
                (lane_hbm, lane_ref),
            )
        )
    ]
    for fetch in fetches:
        fetch.start()
    for fetch in fetches:
        fetch.wait()
    device = lax.axis_index(AXES)
    wide_x, wide_y = box_widths(0)
    per_row = TY // LOW
    base_x = (device // per_row).astype(jnp.float32) * wide_x + 0.5 * wide_x
    base_y = (device % per_row).astype(jnp.float32) * (LOW * wide_y) + 0.5 * wide_y

    which = lax.broadcasted_iota(jnp.int32, (MODES, LANES), 0)
    kx = jnp.zeros((MODES, LANES), jnp.float32)
    ky = jnp.zeros((MODES, LANES), jnp.float32)
    for mode in range(MODES):
        kx = jnp.where(which == mode, speed_ref[0, mode], kx)
        ky = jnp.where(which == mode, speed_ref[1, mode], ky)
    for level in range(BITS + 1):
        at = OFFSET_ROW + 2 * level
        turns = kx * lane_ref[at : at + 1, :] + ky * lane_ref[at + 1 : at + 2, :]
        sine, _ = sin_cos_fine(turns)
        half = turns * horner(SIN_FINE, turns * turns)
        at = level * 2 * MODES
        mode_ref[at : at + MODES, :] = -2.0 * half * half
        mode_ref[at + MODES : at + 2 * MODES, :] = sine
    copy = pltpu.make_async_copy(mode_ref, mode_smem, sems.at[4])
    copy.start()

    low = lax.broadcasted_iota(jnp.int32, (LOW, LANES), 0).astype(jnp.float32) * wide_y
    for mode in range(MODES):
        at_base = (
            speed_ref[0, mode] * base_x
            + speed_ref[1, mode] * base_y
            + shift_ref[mode] * (1.0 / TWO_PI)
        )
        sine, cosine = sin_cos_fine(at_base + speed_ref[1, mode] * low)
        row_ref[mode] = amp_ref[mode] * sine
        row_ref[MODES + mode] = amp_ref[mode] * cosine
    copy.wait()

    def differences(source_ref, level, p, groups):
        even = [[] for _ in range(groups)]
        odd = [[] for _ in range(groups)]
        for mode in range(MODES):
            less = mode_smem[level * 2 * MODES + mode, p]
            sine = mode_smem[level * 2 * MODES + MODES + mode, p]
            for t in range(groups):
                rows = slice(8 * t, 8 * t + 8)
                even[t].append(source_ref[mode, rows, :] * less)
                odd[t].append(source_ref[MODES + mode, rows, :] * sine)
        sums = []
        for t in range(groups):
            x, y = tree_sum(even[t]), tree_sum(odd[t])
            sums.append((x + y, x - y))
        return tuple(sums)

    def put(ref, at, rows, turns):
        sine, cosine = sin_cos(turns)
        ref[at, rows, :] = cosine
        ref[at + 1, rows, :] = sine

    length = lane_ref[FIRST_ROW : FIRST_ROW + 1, :]

    def first_step(p, carry):
        a = p // CHEB
        b = p - a * CHEB
        line = (
            lane_ref[pl.ds(FIRST_ROW + 1 + a, 1), :]
            + lane_ref[pl.ds(FIRST_ROW + 1 + CHEB + b, 1), :]
        )
        back = (
            lane_ref[pl.ds(FIRST_ROW + CHEB - a, 1), :]
            + lane_ref[pl.ds(FIRST_ROW + 2 * CHEB - b, 1), :]
        )
        for t, (here, there) in enumerate(differences(row_ref, BITS, p, LOW // 8)):
            rows = slice(8 * t, 8 * t + 8)
            put(first_ref, 2 * p, rows, here * length + line)
            put(first_ref, 2 * (NODES - 1 - p), rows, there * length + back)
        return carry

    lax.fori_loop(0, NODES // 2 + 1, first_step, 0)

    def table_copy(level):
        return pltpu.make_async_copy(
            table_ref.at[pl.ds(level * LEVEL_TABLE, LEVEL_TABLE)],
            table_hbm.at[pl.ds((level - 1) * LEVEL_TABLE, LEVEL_TABLE)],
            out_sems.at[level],
        )

    table0_copy = pltpu.make_async_copy(
        table_ref.at[pl.ds(0, LEVEL_TABLE)], table0_ref, out_sems.at[0]
    )

    def level_step(level, carry):
        top = level * TABLE
        apart = [lane_ref[pl.ds(top + c, 1), :] for c in range(2)]
        parent = lane_ref[pl.ds(top + 2, 1), :]
        move_x = lane_ref[pl.ds(top + 3, 1), :]
        move_y = lane_ref[pl.ds(top + 4, 1), :]
        for mode in range(MODES):
            sine, cosine = sin_cos_fine(speed_ref[0, mode] * move_x + speed_ref[1, mode] * move_y)
            old_sine = row_ref[mode, :HALF, :]
            old_cosine = row_ref[MODES + mode, :HALF, :]
            wave_ref[mode] = old_sine * cosine + old_cosine * sine
            wave_ref[MODES + mode] = old_cosine * cosine - old_sine * sine
        moved = [
            (here * parent, there * parent)
            for here, there in differences(wave_ref, level, NODES // 2, HALF // 8)
        ]

        def row_step(a, inner_carry):
            lines = [
                (
                    lane_ref[pl.ds(top + 5 + 2 * CHEB * c + a, 1), :],
                    lane_ref[pl.ds(top + 5 + 2 * CHEB * (c + 1) - 1 - a, 1), :],
                )
                for c in range(2)
            ]
            for b in range(CHEB):
                p = a * CHEB + b
                far = differences(wave_ref, level, p, HALF // 8)
                for c in range(2):
                    at = (2 * level + c) * (4 * NODES)
                    for t in range(HALF // 8):
                        rows = slice(8 * t, 8 * t + 8)
                        for k, place in enumerate((2 * p, 2 * (2 * NODES - 1 - p))):
                            turns = far[t][k] * apart[c] + (moved[t][k] + lines[c][k])
                            put(table_ref, at + place, rows, turns)
            return inner_carry

        lax.fori_loop(0, CHEB, row_step, 0)
        return carry

    def later_step(level, carry):
        level_step(level, carry)
        table_copy(level).start()
        return carry

    level_step(0, 0)
    table0_copy.start()
    lax.fori_loop(1, BITS, later_step, 0)
    table0_copy.wait()
    for level in range(1, BITS):
        table_copy(level).wait()


def phases(speed_amp, speed_wave, speed_shift, lanes):
    return pl.pallas_call(
        phase_kernel,
        in_specs=[pl.BlockSpec(memory_space=pltpu.HBM)] * 4,
        out_specs=[
            pl.BlockSpec(memory_space=pltpu.HBM),
            pl.BlockSpec(memory_space=pltpu.VMEM),
            pl.BlockSpec(memory_space=pltpu.VMEM),
        ],
        out_shape=[
            pltpu.HBM(((BITS - 1) * LEVEL_TABLE, HALF, LANES), jnp.float32),
            pltpu.VMEM((LEVEL_TABLE, HALF, LANES), jnp.float32),
            pltpu.VMEM((2 * NODES, LOW, LANES), jnp.float32),
        ],
        scratch_shapes=[
            pltpu.SMEM((MODES,), jnp.float32),
            pltpu.SMEM((2, MODES), jnp.float32),
            pltpu.SMEM((MODES,), jnp.float32),
            pltpu.VMEM(lanes.shape, jnp.float32),
            pltpu.VMEM((BITS * LEVEL_TABLE, HALF, LANES), jnp.float32),
            pltpu.VMEM((2 * MODES, LOW, LANES), jnp.float32),
            pltpu.VMEM((2 * MODES, HALF, LANES), jnp.float32),
            pltpu.VMEM(((BITS + 1) * 2 * MODES, LANES), jnp.float32),
            pltpu.SMEM(((BITS + 1) * 2 * MODES, LANES), jnp.float32),
            pltpu.SemaphoreType.DMA((6,)),
            pltpu.SemaphoreType.DMA((BITS,)),
        ],
        compiler_params=pltpu.CompilerParams(vmem_limit_bytes=32 * 2**20),
        cost_estimate=pl.CostEstimate(
            flops=70 * 10**6, bytes_accessed=13 * 10**6, transcendentals=3 * 10**6
        ),
    )(*map(in_hbm, (speed_amp, speed_wave, speed_shift, lanes)))


def level_kernel(
    got_ref,
    table_hbm,
    table0_ref,
    first_ref,
    out_hbm,
    state_ref,
    other_ref,
    table_ref,
    out_ref,
    slot0_ref,
    slot1_ref,
    sems,
    out_sems,
):
    copies = []
    for level in range(BITS - 1):
        part = pl.ds(level * LEVEL_TABLE, LEVEL_TABLE)
        copies.append(
            pltpu.make_async_copy(table_hbm.at[part], table_ref.at[part], sems.at[level])
        )
    for copy in copies:
        copy.start()
    turn = lax.axis_index(AXES) % PACK

    def unpack(m):
        block = got_ref[pl.ds(m, DEVICES, stride=PACKED), :].T
        for n in range(PACK):
            plane = PACK * m + lax.rem(n + PACK - turn, PACK)
            state_ref[pl.ds(pl.multiple_of(plane * LOW, LOW), LOW), :] = block[
                n * LOW : (n + 1) * LOW, :
            ]

    def unpack_step(k, carry):
        for m in range(3):
            unpack(3 * k + m)
        return carry

    unpack(PACKED - 1)
    lax.fori_loop(0, PACKED // 3, unpack_step, 0)
    lane = lax.broadcasted_iota(jnp.int32, (8, LANES), 1)
    order = lane % 2
    for bit in range(1, BITS):
        order = order + ((lane >> (BITS - bit)) % 2 << bit)

    def places_of(level, b):
        return [a * CHEB + b if split_first(level) else b * CHEB + a for a in range(CHEB)]

    slots = (slot0_ref, slot1_ref)
    states = (state_ref, other_ref)

    def fetch(level, b, t):
        shift = 2 ** LANE_BIT[level]
        low = lane // shift % 2 == 0
        for a, at in enumerate(places_of(level, b)):
            pair = []
            for half in range(2):
                row = half * HALF + 8 * t
                re = states[level % 2][pl.ds(at * LOW + row, 8), :]
                im = states[level % 2][pl.ds((NODES + at) * LOW + row, 8), :]
                if level == 0:
                    rows = slice(row, row + 8)
                    cosine, sine = first_ref[2 * at, rows, :], first_ref[2 * at + 1, rows, :]
                    re, im = re * cosine - im * sine, re * sine + im * cosine
                pair.append((re, im))
            for r in range(2):
                for c, value in enumerate(swap(pair[0][r], pair[1][r], shift, low)):
                    slots[t][(2 * a + r) * 2 + c] = value

    def split(level, b, t, values):
        rows = slice(8 * t, 8 * t + 8)
        places = places_of(level, b)

        def rotated(half, a, near):
            real = imag = None
            for c in range(2):
                table = table_ref if level else table0_ref
                e = 2 * ((2 * c + half) * NODES + a * CHEB + b)
                e = e + max(level - 1, 0) * LEVEL_TABLE
                cosine, sine = table[e, rows, :], table[e + 1, rows, :]
                re, im = near[0][c], near[1][c]
                new_re, new_im = re * cosine - im * sine, re * sine + im * cosine
                real = new_re if c == 0 else real + new_re
                imag = new_im if c == 0 else imag + new_im
            return real, imag

        def keep(a, totals):
            for r in range(2):
                first, second = totals[0][r], totals[1][r]
                if level == BITS - 1:
                    first, second = swap(first, second, 1, lane % 2 == 0)
                    for half, value in enumerate((first, second)):
                        at_row = (half * HALF + 8 * t) * 2 + r
                        out_ref[a, b, pl.ds(at_row, 8, stride=2), :] = jnp.take_along_axis(
                            value, order, axis=1
                        )
                    continue
                at_row = (r * NODES + places[a]) * LOW + 8 * t
                states[1 - level % 2][pl.ds(at_row, 8), :] = first
                states[1 - level % 2][pl.ds(at_row + HALF, 8), :] = second

        ends = [[[values[a][r][c] for c in range(2)] for r in range(2)] for a in (0, 2, 4)]
        keep(0, (rotated(0, 0, ends[1]), rotated(1, 0, ends[0])))
        keep(4, (rotated(0, 4, ends[2]), rotated(1, 4, ends[1])))
        parts = [
            [
                (
                    values[0][r][c] + values[4][r][c],
                    values[1][r][c] + values[3][r][c],
                    values[0][r][c] - values[4][r][c],
                    values[1][r][c] - values[3][r][c],
                    values[2][r][c],
                )
                for c in range(2)
            ]
            for r in range(2)
        ]
        _, child = points_of()
        held = {}
        for i in range(1, CHEB - 1):
            row = lagrange_of(child[0, i])
            sums, gaps = [[], []], [[], []]
            for r in range(2):
                for c in range(2):
                    even0, even1, odd0, odd1, middle = parts[r][c]
                    even = (
                        float((row[0] + row[4]) / 2) * even0
                        + float((row[1] + row[3]) / 2) * even1
                        + float(row[2]) * middle
                    )
                    odd = (
                        float((row[0] - row[4]) / 2) * odd0
                        + float((row[1] - row[3]) / 2) * odd1
                    )
                    sums[r].append(even + odd)
                    gaps[r].append(even - odd)
            held[0, i] = rotated(0, i, sums)
            held[1, CHEB - 1 - i] = rotated(1, CHEB - 1 - i, gaps)
            for a in range(1, CHEB - 1):
                if (0, a) in held and (1, a) in held:
                    keep(a, (held.pop((0, a)), held.pop((1, a))))

    def out_copy(b):
        return pltpu.make_async_copy(out_ref.at[:, b], out_hbm.at[:, b], out_sems.at[b])

    for level in range(BITS):
        if level:
            copies[level - 1].wait()
        for t in range(HALF // 8):
            fetch(level, 0, t)

        def step(b, carry, level=level):
            for t in range(HALF // 8):
                values = [
                    [[slots[t][(2 * a + r) * 2 + c] for c in range(2)] for r in range(2)]
                    for a in range(CHEB)
                ]
                fetch(level, jnp.minimum(b + 1, CHEB - 1), t)
                split(level, b, t, values)
            if level == BITS - 1:
                out_copy(b).start()
            return carry

        lax.fori_loop(0, CHEB, step, 0)
    for b in range(CHEB):
        out_copy(b).wait()


def levels(got, table, table0, first):
    return pl.pallas_call(
        level_kernel,
        in_specs=[
            pl.BlockSpec(memory_space=pltpu.VMEM),
            pl.BlockSpec(memory_space=pltpu.HBM),
            pl.BlockSpec(memory_space=pltpu.VMEM),
            pl.BlockSpec(memory_space=pltpu.VMEM),
        ],
        out_specs=pl.BlockSpec(memory_space=pltpu.HBM),
        out_shape=pltpu.HBM((CHEB, CHEB, 2 * LOW, LANES), jnp.float32),
        scratch_shapes=[
            pltpu.VMEM((PACK * PACKED * LOW, LANES), jnp.float32),
            pltpu.VMEM((PLANES * LOW, LANES), jnp.float32),
            pltpu.VMEM(((BITS - 1) * LEVEL_TABLE, HALF, LANES), jnp.float32),
            pltpu.VMEM((CHEB, CHEB, 2 * LOW, LANES), jnp.float32),
            pltpu.VMEM((4 * CHEB, 8, LANES), jnp.float32),
            pltpu.VMEM((4 * CHEB, 8, LANES), jnp.float32),
            pltpu.SemaphoreType.DMA((BITS - 1,)),
            pltpu.SemaphoreType.DMA((CHEB,)),
        ],
        compiler_params=pltpu.CompilerParams(vmem_limit_bytes=32 * 2**20),
        cost_estimate=pl.CostEstimate(
            flops=22 * 10**6, bytes_accessed=14 * 10**6, transcendentals=0
        ),
    )(got, in_hbm(table), table0, first)


def on_device(coefficients, speed_amp, speed_wave, speed_shift):
    packed = pack(coefficients.reshape(PLANES, DEVICES // PACK, LANES))
    sent = packed.reshape(DEVICES, 1, PACKED * LANES)
    got = lax.all_to_all(sent, AXES, 0, 0, tiled=True)
    got = got.reshape(DEVICES * PACKED, LANES)
    table, table0, first = phases(speed_amp, speed_wave, speed_shift, jnp.asarray(lane_tables()))
    final = levels(got, table, table0, first).reshape(CHEB, CHEB, LOW, 2, LANES)
    return final.transpose(3, 0, 1, 2, 4).reshape(2, CHEB, CHEB, LOW * LANES)


def solution(mesh):
    in_specs = (P(None, None, None, AXES, None), P(), P(), P())
    out_specs = P(None, None, None, AXES)
    return jax.shard_map(
        on_device, mesh=mesh, in_specs=in_specs, out_specs=out_specs, check_vma=False
    )
```

```python
import math

import jax
import jax.numpy as jnp
import numpy as np
from jax import lax
from jax.experimental import pallas as pl
from jax.experimental.pallas import tpu as pltpu
from jax.sharding import PartitionSpec as P

N = 16384
CHEB = 5
MODES = 8
TX = 32
TY = 128
BITS = 7
DEVICES = 128
LANES = 128
NODES = CHEB * CHEB
PLANES = 2 * NODES
LOW = TX * TY // DEVICES
HALF = LOW // 2
PACK = LANES // LOW
PACKED = -(-PLANES // PACK)
LANE_BIT = (0, 1, 2, 3, 4, 5, 6)
LEVEL_TABLE = 8 * NODES
TABLE = 25
FIRST_ROW = BITS * TABLE
OFFSET_ROW = FIRST_ROW + 1 + 2 * CHEB
TWO_PI = 2.0 * math.pi
ROUND = 1.5 * 2.0**23
AXES = ("outer", "inner")


def split_first(level):
    return (BITS - 1 - level) % 2 == 0


def box_widths(level):
    splits_x = sum(1 for bit in range(BITS) if split_first(bit))
    splits_y = BITS - splits_x
    before_x = sum(1 for bit in range(level) if split_first(bit))
    before_y = level - before_x
    return (2.0**splits_x / N / 2.0**before_x, 2.0**splits_y / N / 2.0**before_y)


def points_of():
    points = 0.5 * np.cos(np.arange(CHEB) * np.pi / (CHEB - 1))
    child = np.stack([(half - 0.5) / 2.0 + points / 2.0 for half in (0, 1)])
    return points, child


def lagrange_of(u):
    points, _ = points_of()
    row = np.ones(CHEB)
    for j in range(CHEB):
        for m in range(CHEB):
            if m != j:
                row[j] *= (u - points[m]) / (points[j] - points[m])
    return row


def source_centre(ids, level):
    freq_x = np.zeros(len(ids))
    freq_y = np.zeros(len(ids))
    for bit in range(level, BITS):
        sign = (ids >> bit) % 2 - 0.5
        depth = (BITS - 1 - bit) // 2 + 1
        if split_first(bit):
            freq_x = freq_x + sign * (N / 2.0**depth)
        else:
            freq_y = freq_y + sign * (N / 2.0**depth)
    return freq_x, freq_y


def lane_tables():
    points, child = points_of()
    lane = np.arange(LANES)
    bit_of = [(lane >> LANE_BIT[k]) % 2 for k in range(BITS)]
    rows = []
    for level in range(BITS):
        width = box_widths(level)[0 if split_first(level) else 1]
        parent_id = sum(bit_of[k] << k for k in range(level + 1, BITS)) + 0 * lane
        parent_x, parent_y = source_centre(parent_id, level + 1)
        parent = np.sqrt(parent_x**2 + parent_y**2)
        centres = [source_centre(parent_id + (c << level), level) for c in range(2)]
        move_x = np.zeros(LANES)
        move_y = (lane % 2) * (HALF * box_widths(0)[1])
        for k in range(level):
            wide_x, wide_y = box_widths(k)
            half = (bit_of[k + 1] - 0.5) / 2.0
            if split_first(k):
                move_x = move_x + half * wide_x
            else:
                move_y = move_y + half * wide_y
        for c in range(2):
            rows.append(np.sqrt(centres[c][0] ** 2 + centres[c][1] ** 2) - parent)
        rows += [parent, move_x, move_y]
        for c in range(2):
            own_d, parent_d = (
                (centres[c][0], parent_x) if split_first(level) else (centres[c][1], parent_y)
            )
            for half in range(2):
                for i in range(CHEB):
                    turn = width * child[half, i] * own_d - width * points[i] / 2.0 * parent_d
                    rows.append(turn - np.round(turn))
    source = sum(bit_of[k] << k for k in range(BITS))
    freq_x, freq_y = source_centre(source, 0)
    wide_x, wide_y = box_widths(0)
    rows.append(-np.sqrt(freq_x**2 + freq_y**2))
    for i in range(CHEB):
        turn = -wide_x * points[i] * freq_x
        rows.append(turn - np.round(turn))
    for j in range(CHEB):
        turn = -wide_y * points[j] * freq_y
        rows.append(turn - np.round(turn))
    off_x, off_y = offset_tables()
    for level in range(BITS + 1):
        rows += [off_x[level], off_y[level]]
    while len(rows) % 8:
        rows.append(np.zeros(LANES))
    return np.stack(rows).astype(np.float32)


def offset_tables():
    points, child = points_of()
    off_x = np.zeros((BITS + 1, LANES))
    off_y = np.zeros((BITS + 1, LANES))
    for level in range(BITS + 1):
        wide_x, wide_y = box_widths(level % BITS)
        for a in range(CHEB):
            for b in range(CHEB):
                p = a * CHEB + b
                if level == BITS:
                    off_x[level, p], off_y[level, p] = wide_x * points[a], wide_y * points[b]
                elif split_first(level):
                    off_x[level, p], off_y[level, p] = wide_x * child[0, a], wide_y * points[b]
                else:
                    off_x[level, p], off_y[level, p] = wide_x * points[b], wide_y * child[0, a]
    return off_x, off_y


def chebyshev_fit(function, odd, terms):
    grid = 0.5 * np.cos((np.arange(400) + 0.5) * np.pi / 400)
    powers = np.stack([grid ** (2 * k + (1 if odd else 0)) for k in range(terms)], axis=1)
    answer, *_ = np.linalg.lstsq(powers, function(math.pi * grid), rcond=None)
    return [float(v) for v in answer]


SIN_FIT = chebyshev_fit(np.sin, True, 4)
COS_FIT = chebyshev_fit(np.cos, False, 5)
SIN_FINE = chebyshev_fit(np.sin, True, 6)
COS_FINE = chebyshev_fit(np.cos, False, 6)


def horner(fit, square):
    total = fit[-1]
    for value in fit[-2::-1]:
        total = total * square + value
    return total


def sin_cos(turns, sin_fit=SIN_FIT, cos_fit=COS_FIT):
    turns = turns - ((turns + ROUND) - ROUND)
    square = turns * turns
    sine = turns * horner(sin_fit, square)
    twice = sine + sine
    return twice * horner(cos_fit, square), 1.0 - twice * sine


def sin_cos_fine(turns):
    return sin_cos(turns, SIN_FINE, COS_FINE)


def swap(left, right, shift, low):
    lane = lax.broadcasted_iota(jnp.int32, left.shape, 1)
    moved = jnp.take_along_axis(
        jnp.where(low, right, left), jnp.bitwise_xor(lane, shift), axis=1
    )
    return jnp.where(low, left, moved), jnp.where(low, moved, right)


def in_hbm(value):
    return pltpu.with_memory_space_constraint(value, pltpu.HBM)


def pack_kernel(planes_hbm, out_hbm, in_ref, out_ref, in_sems, out_sems):
    lane = lax.broadcasted_iota(jnp.int32, (8, LANES), 1)
    high = lane >= 2 * LOW
    odd = lane % (2 * LOW) >= LOW
    groups = planes_hbm.shape[1] // 8

    def fetch(g):
        rows = pl.ds(pl.multiple_of(8 * g, 8), 8)
        return pltpu.make_async_copy(planes_hbm.at[:, rows, :], in_ref.at[g], in_sems.at[g])

    def store(g):
        part = pl.ds(pl.multiple_of(g * size, 8), size)
        return pltpu.make_async_copy(out_ref.at[part], out_hbm.at[part], out_sems.at[g])

    def group_step(g, carry):
        fetch(g).wait()
        for m in range(PACKED):
            blocks = [in_ref[g, min(PACK * m + n, PLANES - 1)] for n in range(PACK)]
            blocks = [
                pltpu.roll(block, n * LOW, 1) if n else block for n, block in enumerate(blocks)
            ]
            for r in range(PACK):
                part = [blocks[(k - r) % PACK] for k in range(PACK)]
                turned = jnp.where(
                    high,
                    jnp.where(odd, part[3], part[2]),
                    jnp.where(odd, part[1], part[0]),
                )
                out_ref[pl.ds(g * size + r * PACKED + m, 8, stride=PACK * PACKED), :] = turned
        store(g).start()
        return carry

    size = 8 * PACK * PACKED
    for g in range(groups):
        fetch(g).start()
    lax.fori_loop(0, groups, group_step, 0)
    for g in range(groups):
        store(g).wait()


def pack(planes):
    groups = planes.shape[1] // 8
    return pl.pallas_call(
        pack_kernel,
        in_specs=[pl.BlockSpec(memory_space=pltpu.HBM)],
        out_specs=pl.BlockSpec(memory_space=pltpu.HBM),
        out_shape=pltpu.HBM((DEVICES * PACKED, LANES), jnp.float32),
        scratch_shapes=[
            pltpu.VMEM((groups, PLANES, 8, LANES), jnp.float32),
            pltpu.VMEM((DEVICES * PACKED, LANES), jnp.float32),
            pltpu.SemaphoreType.DMA((groups,)),
            pltpu.SemaphoreType.DMA((groups,)),
        ],
        compiler_params=pltpu.CompilerParams(vmem_limit_bytes=16 * 2**20),
        cost_estimate=pl.CostEstimate(flops=10**6, bytes_accessed=1700000, transcendentals=0),
    )(in_hbm(planes))


def tree_sum(terms):
    while len(terms) > 1:
        terms = [terms[k] + terms[k + 1] for k in range(0, len(terms), 2)]
    return terms[0]


def phase_kernel(
    amp_hbm,
    speed_hbm,
    shift_hbm,
    lane_hbm,
    table_hbm,
    table0_ref,
    first_ref,
    amp_ref,
    speed_ref,
    shift_ref,
    lane_ref,
    table_ref,
    row_ref,
    wave_ref,
    mode_ref,
    mode_smem,
    sems,
    out_sems,
):
    fetches = [
        pltpu.make_async_copy(source, target, sems.at[k])
        for k, (source, target) in enumerate(
            (
                (amp_hbm, amp_ref),
                (speed_hbm, speed_ref),
                (shift_hbm, shift_ref),
                (lane_hbm, lane_ref),
            )
        )
    ]
    for fetch in fetches:
        fetch.start()
    for fetch in fetches:
        fetch.wait()
    device = lax.axis_index(AXES)
    wide_x, wide_y = box_widths(0)
    per_row = TY // LOW
    base_x = (device // per_row).astype(jnp.float32) * wide_x + 0.5 * wide_x
    base_y = (device % per_row).astype(jnp.float32) * (LOW * wide_y) + 0.5 * wide_y

    which = lax.broadcasted_iota(jnp.int32, (MODES, LANES), 0)
    kx = jnp.zeros((MODES, LANES), jnp.float32)
    ky = jnp.zeros((MODES, LANES), jnp.float32)
    for mode in range(MODES):
        kx = jnp.where(which == mode, speed_ref[0, mode], kx)
        ky = jnp.where(which == mode, speed_ref[1, mode], ky)
    for level in range(BITS + 1):
        at = OFFSET_ROW + 2 * level
        turns = kx * lane_ref[at : at + 1, :] + ky * lane_ref[at + 1 : at + 2, :]
        sine, _ = sin_cos_fine(turns)
        half = turns * horner(SIN_FINE, turns * turns)
        at = level * 2 * MODES
        mode_ref[at : at + MODES, :] = -2.0 * half * half
        mode_ref[at + MODES : at + 2 * MODES, :] = sine
    copy = pltpu.make_async_copy(mode_ref, mode_smem, sems.at[4])
    copy.start()

    low = lax.broadcasted_iota(jnp.int32, (LOW, LANES), 0).astype(jnp.float32) * wide_y
    for mode in range(MODES):
        at_base = (
            speed_ref[0, mode] * base_x
            + speed_ref[1, mode] * base_y
            + shift_ref[mode] * (1.0 / TWO_PI)
        )
        sine, cosine = sin_cos_fine(at_base + speed_ref[1, mode] * low)
        row_ref[mode] = amp_ref[mode] * sine
        row_ref[MODES + mode] = amp_ref[mode] * cosine
    copy.wait()

    def differences(source_ref, level, p, groups):
        even = [[] for _ in range(groups)]
        odd = [[] for _ in range(groups)]
        for mode in range(MODES):
            less = mode_smem[level * 2 * MODES + mode, p]
            sine = mode_smem[level * 2 * MODES + MODES + mode, p]
            for t in range(groups):
                rows = slice(8 * t, 8 * t + 8)
                even[t].append(source_ref[mode, rows, :] * less)
                odd[t].append(source_ref[MODES + mode, rows, :] * sine)
        sums = []
        for t in range(groups):
            x, y = tree_sum(even[t]), tree_sum(odd[t])
            sums.append((x + y, x - y))
        return tuple(sums)

    def put(ref, at, rows, turns):
        sine, cosine = sin_cos(turns)
        ref[at, rows, :] = cosine
        ref[at + 1, rows, :] = sine

    length = lane_ref[FIRST_ROW : FIRST_ROW + 1, :]

    def first_step(p, carry):
        a = p // CHEB
        b = p - a * CHEB
        line = (
            lane_ref[pl.ds(FIRST_ROW + 1 + a, 1), :]
            + lane_ref[pl.ds(FIRST_ROW + 1 + CHEB + b, 1), :]
        )
        back = (
            lane_ref[pl.ds(FIRST_ROW + CHEB - a, 1), :]
            + lane_ref[pl.ds(FIRST_ROW + 2 * CHEB - b, 1), :]
        )
        for t, (here, there) in enumerate(differences(row_ref, BITS, p, LOW // 8)):
            rows = slice(8 * t, 8 * t + 8)
            put(first_ref, 2 * p, rows, here * length + line)
            put(first_ref, 2 * (NODES - 1 - p), rows, there * length + back)
        return carry

    lax.fori_loop(0, NODES // 2 + 1, first_step, 0)

    def table_copy(level):
        return pltpu.make_async_copy(
            table_ref.at[pl.ds(level * LEVEL_TABLE, LEVEL_TABLE)],
            table_hbm.at[pl.ds((level - 1) * LEVEL_TABLE, LEVEL_TABLE)],
            out_sems.at[level],
        )

    table0_copy = pltpu.make_async_copy(
        table_ref.at[pl.ds(0, LEVEL_TABLE)], table0_ref, out_sems.at[0]
    )

    def level_step(level, carry):
        top = level * TABLE
        apart = [lane_ref[pl.ds(top + c, 1), :] for c in range(2)]
        parent = lane_ref[pl.ds(top + 2, 1), :]
        move_x = lane_ref[pl.ds(top + 3, 1), :]
        move_y = lane_ref[pl.ds(top + 4, 1), :]
        for mode in range(MODES):
            sine, cosine = sin_cos_fine(speed_ref[0, mode] * move_x + speed_ref[1, mode] * move_y)
            old_sine = row_ref[mode, :HALF, :]
            old_cosine = row_ref[MODES + mode, :HALF, :]
            wave_ref[mode] = old_sine * cosine + old_cosine * sine
            wave_ref[MODES + mode] = old_cosine * cosine - old_sine * sine
        moved = [
            (here * parent, there * parent)
            for here, there in differences(wave_ref, level, NODES // 2, HALF // 8)
        ]

        def row_step(a, inner_carry):
            lines = [
                (
                    lane_ref[pl.ds(top + 5 + 2 * CHEB * c + a, 1), :],
                    lane_ref[pl.ds(top + 5 + 2 * CHEB * (c + 1) - 1 - a, 1), :],
                )
                for c in range(2)
            ]
            for b in range(CHEB):
                p = a * CHEB + b
                far = differences(wave_ref, level, p, HALF // 8)
                for c in range(2):
                    at = (2 * level + c) * (4 * NODES)
                    for t in range(HALF // 8):
                        rows = slice(8 * t, 8 * t + 8)
                        for k, place in enumerate((2 * p, 2 * (2 * NODES - 1 - p))):
                            turns = far[t][k] * apart[c] + (moved[t][k] + lines[c][k])
                            put(table_ref, at + place, rows, turns)
            return inner_carry

        lax.fori_loop(0, CHEB, row_step, 0)
        return carry

    def later_step(level, carry):
        level_step(level, carry)
        table_copy(level).start()
        return carry

    level_step(0, 0)
    table0_copy.start()
    lax.fori_loop(1, BITS, later_step, 0)
    table0_copy.wait()
    for level in range(1, BITS):
        table_copy(level).wait()


def phases(speed_amp, speed_wave, speed_shift, lanes):
    return pl.pallas_call(
        phase_kernel,
        in_specs=[pl.BlockSpec(memory_space=pltpu.HBM)] * 4,
        out_specs=[
            pl.BlockSpec(memory_space=pltpu.HBM),
            pl.BlockSpec(memory_space=pltpu.VMEM),
            pl.BlockSpec(memory_space=pltpu.VMEM),
        ],
        out_shape=[
            pltpu.HBM(((BITS - 1) * LEVEL_TABLE, HALF, LANES), jnp.float32),
            pltpu.VMEM((LEVEL_TABLE, HALF, LANES), jnp.float32),
            pltpu.VMEM((2 * NODES, LOW, LANES), jnp.float32),
        ],
        scratch_shapes=[
            pltpu.SMEM((MODES,), jnp.float32),
            pltpu.SMEM((2, MODES), jnp.float32),
            pltpu.SMEM((MODES,), jnp.float32),
            pltpu.VMEM(lanes.shape, jnp.float32),
            pltpu.VMEM((BITS * LEVEL_TABLE, HALF, LANES), jnp.float32),
            pltpu.VMEM((2 * MODES, LOW, LANES), jnp.float32),
            pltpu.VMEM((2 * MODES, HALF, LANES), jnp.float32),
            pltpu.VMEM(((BITS + 1) * 2 * MODES, LANES), jnp.float32),
            pltpu.SMEM(((BITS + 1) * 2 * MODES, LANES), jnp.float32),
            pltpu.SemaphoreType.DMA((6,)),
            pltpu.SemaphoreType.DMA((BITS,)),
        ],
        compiler_params=pltpu.CompilerParams(vmem_limit_bytes=32 * 2**20),
        cost_estimate=pl.CostEstimate(
            flops=70 * 10**6, bytes_accessed=13 * 10**6, transcendentals=3 * 10**6
        ),
    )(*map(in_hbm, (speed_amp, speed_wave, speed_shift, lanes)))


def level_kernel(
    got_ref,
    table_hbm,
    table0_ref,
    first_ref,
    out_hbm,
    state_ref,
    other_ref,
    table_ref,
    out_ref,
    slot0_ref,
    slot1_ref,
    sems,
    out_sems,
):
    copies = []
    for level in range(BITS - 1):
        part = pl.ds(level * LEVEL_TABLE, LEVEL_TABLE)
        copies.append(
            pltpu.make_async_copy(table_hbm.at[part], table_ref.at[part], sems.at[level])
        )
    for copy in copies:
        copy.start()
    turn = lax.axis_index(AXES) % PACK

    def unpack(m):
        block = got_ref[pl.ds(m, DEVICES, stride=PACKED), :].T
        for n in range(PACK):
            plane = PACK * m + lax.rem(n + PACK - turn, PACK)
            state_ref[pl.ds(pl.multiple_of(plane * LOW, LOW), LOW), :] = block[
                n * LOW : (n + 1) * LOW, :
            ]

    def unpack_step(k, carry):
        for m in range(3):
            unpack(3 * k + m)
        return carry

    unpack(PACKED - 1)
    lax.fori_loop(0, PACKED // 3, unpack_step, 0)
    lane = lax.broadcasted_iota(jnp.int32, (8, LANES), 1)
    order = lane % 2
    for bit in range(1, BITS):
        order = order + ((lane >> (BITS - bit)) % 2 << bit)

    def places_of(level, b):
        return [a * CHEB + b if split_first(level) else b * CHEB + a for a in range(CHEB)]

    slots = (slot0_ref, slot1_ref)
    states = (state_ref, other_ref)

    def fetch(level, b, t):
        shift = 2 ** LANE_BIT[level]
        low = lane // shift % 2 == 0
        for a, at in enumerate(places_of(level, b)):
            pair = []
            for half in range(2):
                row = half * HALF + 8 * t
                re = states[level % 2][pl.ds(at * LOW + row, 8), :]
                im = states[level % 2][pl.ds((NODES + at) * LOW + row, 8), :]
                if level == 0:
                    rows = slice(row, row + 8)
                    cosine, sine = first_ref[2 * at, rows, :], first_ref[2 * at + 1, rows, :]
                    re, im = re * cosine - im * sine, re * sine + im * cosine
                pair.append((re, im))
            for r in range(2):
                for c, value in enumerate(swap(pair[0][r], pair[1][r], shift, low)):
                    slots[t][(2 * a + r) * 2 + c] = value

    def split(level, b, t, values):
        rows = slice(8 * t, 8 * t + 8)
        places = places_of(level, b)

        def rotated(half, a, near):
            real = imag = None
            for c in range(2):
                table = table_ref if level else table0_ref
                e = 2 * ((2 * c + half) * NODES + a * CHEB + b)
                e = e + max(level - 1, 0) * LEVEL_TABLE
                cosine, sine = table[e, rows, :], table[e + 1, rows, :]
                re, im = near[0][c], near[1][c]
                new_re, new_im = re * cosine - im * sine, re * sine + im * cosine
                real = new_re if c == 0 else real + new_re
                imag = new_im if c == 0 else imag + new_im
            return real, imag

        def keep(a, totals):
            for r in range(2):
                first, second = totals[0][r], totals[1][r]
                if level == BITS - 1:
                    first, second = swap(first, second, 1, lane % 2 == 0)
                    for half, value in enumerate((first, second)):
                        at_row = (half * HALF + 8 * t) * 2 + r
                        out_ref[a, b, pl.ds(at_row, 8, stride=2), :] = jnp.take_along_axis(
                            value, order, axis=1
                        )
                    continue
                at_row = (r * NODES + places[a]) * LOW + 8 * t
                states[1 - level % 2][pl.ds(at_row, 8), :] = first
                states[1 - level % 2][pl.ds(at_row + HALF, 8), :] = second

        ends = [[[values[a][r][c] for c in range(2)] for r in range(2)] for a in (0, 2, 4)]
        keep(0, (rotated(0, 0, ends[1]), rotated(1, 0, ends[0])))
        keep(4, (rotated(0, 4, ends[2]), rotated(1, 4, ends[1])))
        parts = [
            [
                (
                    values[0][r][c] + values[4][r][c],
                    values[1][r][c] + values[3][r][c],
                    values[0][r][c] - values[4][r][c],
                    values[1][r][c] - values[3][r][c],
                    values[2][r][c],
                )
                for c in range(2)
            ]
            for r in range(2)
        ]
        _, child = points_of()
        held = {}
        for i in range(1, CHEB - 1):
            row = lagrange_of(child[0, i])
            sums, gaps = [[], []], [[], []]
            for r in range(2):
                for c in range(2):
                    even0, even1, odd0, odd1, middle = parts[r][c]
                    even = (
                        float((row[0] + row[4]) / 2) * even0
                        + float((row[1] + row[3]) / 2) * even1
                        + float(row[2]) * middle
                    )
                    odd = (
                        float((row[0] - row[4]) / 2) * odd0
                        + float((row[1] - row[3]) / 2) * odd1
                    )
                    sums[r].append(even + odd)
                    gaps[r].append(even - odd)
            held[0, i] = rotated(0, i, sums)
            held[1, CHEB - 1 - i] = rotated(1, CHEB - 1 - i, gaps)
            for a in range(1, CHEB - 1):
                if (0, a) in held and (1, a) in held:
                    keep(a, (held.pop((0, a)), held.pop((1, a))))

    def out_copy(b):
        return pltpu.make_async_copy(out_ref.at[:, b], out_hbm.at[:, b], out_sems.at[b])

    for level in range(BITS):
        if level:
            copies[level - 1].wait()
        for t in range(HALF // 8):
            fetch(level, 0, t)

        def step(b, carry, level=level):
            for t in range(HALF // 8):
                values = [
                    [[slots[t][(2 * a + r) * 2 + c] for c in range(2)] for r in range(2)]
                    for a in range(CHEB)
                ]
                fetch(level, jnp.minimum(b + 1, CHEB - 1), t)
                split(level, b, t, values)
            if level == BITS - 1:
                out_copy(b).start()
            return carry

        lax.fori_loop(0, CHEB, step, 0)
    for b in range(CHEB):
        out_copy(b).wait()


def levels(got, table, table0, first):
    return pl.pallas_call(
        level_kernel,
        in_specs=[
            pl.BlockSpec(memory_space=pltpu.VMEM),
            pl.BlockSpec(memory_space=pltpu.HBM),
            pl.BlockSpec(memory_space=pltpu.VMEM),
            pl.BlockSpec(memory_space=pltpu.VMEM),
        ],
        out_specs=pl.BlockSpec(memory_space=pltpu.HBM),
        out_shape=pltpu.HBM((CHEB, CHEB, 2 * LOW, LANES), jnp.float32),
        scratch_shapes=[
            pltpu.VMEM((PACK * PACKED * LOW, LANES), jnp.float32),
            pltpu.VMEM((PLANES * LOW, LANES), jnp.float32),
            pltpu.VMEM(((BITS - 1) * LEVEL_TABLE, HALF, LANES), jnp.float32),
            pltpu.VMEM((CHEB, CHEB, 2 * LOW, LANES), jnp.float32),
            pltpu.VMEM((4 * CHEB, 8, LANES), jnp.float32),
            pltpu.VMEM((4 * CHEB, 8, LANES), jnp.float32),
            pltpu.SemaphoreType.DMA((BITS - 1,)),
            pltpu.SemaphoreType.DMA((CHEB,)),
        ],
        compiler_params=pltpu.CompilerParams(vmem_limit_bytes=32 * 2**20),
        cost_estimate=pl.CostEstimate(
            flops=22 * 10**6, bytes_accessed=14 * 10**6, transcendentals=0
        ),
    )(got, in_hbm(table), table0, first)


def on_device(coefficients, speed_amp, speed_wave, speed_shift):
    packed = pack(coefficients.reshape(PLANES, DEVICES // PACK, LANES))
    sent = packed.reshape(DEVICES, 1, PACKED * LANES)
    got = lax.all_to_all(sent, AXES, 0, 0, tiled=True)
    got = got.reshape(DEVICES * PACKED, LANES)
    table, table0, first = phases(speed_amp, speed_wave, speed_shift, jnp.asarray(lane_tables()))
    final = levels(got, table, table0, first).reshape(CHEB, CHEB, LOW, 2, LANES)
    return final.transpose(3, 0, 1, 2, 4).reshape(2, CHEB, CHEB, LOW * LANES)


def solution(mesh):
    in_specs = (P(None, None, None, AXES, None), P(), P(), P())
    out_specs = P(None, None, None, AXES)
    return jax.shard_map(
        on_device, mesh=mesh, in_specs=in_specs, out_specs=out_specs, check_vma=False
    )
```

```python
import math

import jax
import jax.numpy as jnp
import numpy as np
from jax import lax
from jax.experimental import pallas as pl
from jax.experimental.pallas import tpu as pltpu
from jax.sharding import PartitionSpec as P

N = 16384
CHEB = 5
MODES = 8
TX = 32
TY = 128
BITS = 7
DEVICES = 128
LANES = 128
NODES = CHEB * CHEB
PLANES = 2 * NODES
LOW = TX * TY // DEVICES
HALF = LOW // 2
PACK = LANES // LOW
PACKED = -(-PLANES // PACK)
LANE_BIT = (0, 1, 2, 3, 4, 5, 6)
LEVEL_TABLE = 8 * NODES
TABLE = 25
FIRST_ROW = BITS * TABLE
OFFSET_ROW = FIRST_ROW + 1 + 2 * CHEB
TWO_PI = 2.0 * math.pi
ROUND = 1.5 * 2.0**23
AXES = ("outer", "inner")


def split_first(level):
    return (BITS - 1 - level) % 2 == 0


def box_widths(level):
    splits_x = sum(1 for bit in range(BITS) if split_first(bit))
    splits_y = BITS - splits_x
    before_x = sum(1 for bit in range(level) if split_first(bit))
    before_y = level - before_x
    return (2.0**splits_x / N / 2.0**before_x, 2.0**splits_y / N / 2.0**before_y)


def points_of():
    points = 0.5 * np.cos(np.arange(CHEB) * np.pi / (CHEB - 1))
    child = np.stack([(half - 0.5) / 2.0 + points / 2.0 for half in (0, 1)])
    return points, child


def lagrange_of(u):
    points, _ = points_of()
    row = np.ones(CHEB)
    for j in range(CHEB):
        for m in range(CHEB):
            if m != j:
                row[j] *= (u - points[m]) / (points[j] - points[m])
    return row


def source_centre(ids, level):
    freq_x = np.zeros(len(ids))
    freq_y = np.zeros(len(ids))
    for bit in range(level, BITS):
        sign = (ids >> bit) % 2 - 0.5
        depth = (BITS - 1 - bit) // 2 + 1
        if split_first(bit):
            freq_x = freq_x + sign * (N / 2.0**depth)
        else:
            freq_y = freq_y + sign * (N / 2.0**depth)
    return freq_x, freq_y


def lane_tables():
    points, child = points_of()
    lane = np.arange(LANES)
    bit_of = [(lane >> LANE_BIT[k]) % 2 for k in range(BITS)]
    rows = []
    for level in range(BITS):
        width = box_widths(level)[0 if split_first(level) else 1]
        parent_id = sum(bit_of[k] << k for k in range(level + 1, BITS)) + 0 * lane
        parent_x, parent_y = source_centre(parent_id, level + 1)
        parent = np.sqrt(parent_x**2 + parent_y**2)
        centres = [source_centre(parent_id + (c << level), level) for c in range(2)]
        move_x = np.zeros(LANES)
        move_y = (lane % 2) * (HALF * box_widths(0)[1])
        for k in range(level):
            wide_x, wide_y = box_widths(k)
            half = (bit_of[k + 1] - 0.5) / 2.0
            if split_first(k):
                move_x = move_x + half * wide_x
            else:
                move_y = move_y + half * wide_y
        for c in range(2):
            rows.append(np.sqrt(centres[c][0] ** 2 + centres[c][1] ** 2) - parent)
        rows += [parent, move_x, move_y]
        for c in range(2):
            own_d, parent_d = (
                (centres[c][0], parent_x) if split_first(level) else (centres[c][1], parent_y)
            )
            for half in range(2):
                for i in range(CHEB):
                    turn = width * child[half, i] * own_d - width * points[i] / 2.0 * parent_d
                    rows.append(turn - np.round(turn))
    source = sum(bit_of[k] << k for k in range(BITS))
    freq_x, freq_y = source_centre(source, 0)
    wide_x, wide_y = box_widths(0)
    rows.append(-np.sqrt(freq_x**2 + freq_y**2))
    for i in range(CHEB):
        turn = -wide_x * points[i] * freq_x
        rows.append(turn - np.round(turn))
    for j in range(CHEB):
        turn = -wide_y * points[j] * freq_y
        rows.append(turn - np.round(turn))
    off_x, off_y = offset_tables()
    for level in range(BITS + 1):
        rows += [off_x[level], off_y[level]]
    while len(rows) % 8:
        rows.append(np.zeros(LANES))
    return np.stack(rows).astype(np.float32)


def offset_tables():
    points, child = points_of()
    off_x = np.zeros((BITS + 1, LANES))
    off_y = np.zeros((BITS + 1, LANES))
    for level in range(BITS + 1):
        wide_x, wide_y = box_widths(level % BITS)
        for a in range(CHEB):
            for b in range(CHEB):
                p = a * CHEB + b
                if level == BITS:
                    off_x[level, p], off_y[level, p] = wide_x * points[a], wide_y * points[b]
                elif split_first(level):
                    off_x[level, p], off_y[level, p] = wide_x * child[0, a], wide_y * points[b]
                else:
                    off_x[level, p], off_y[level, p] = wide_x * points[b], wide_y * child[0, a]
    return off_x, off_y


def chebyshev_fit(function, odd, terms):
    grid = 0.5 * np.cos((np.arange(400) + 0.5) * np.pi / 400)
    powers = np.stack([grid ** (2 * k + (1 if odd else 0)) for k in range(terms)], axis=1)
    answer, *_ = np.linalg.lstsq(powers, function(math.pi * grid), rcond=None)
    return [float(v) for v in answer]


SIN_FIT = chebyshev_fit(np.sin, True, 4)
COS_FIT = chebyshev_fit(np.cos, False, 5)
SIN_FINE = chebyshev_fit(np.sin, True, 6)
COS_FINE = chebyshev_fit(np.cos, False, 6)


def horner(fit, square):
    total = fit[-1]
    for value in fit[-2::-1]:
        total = total * square + value
    return total


def sin_cos(turns, sin_fit=SIN_FIT, cos_fit=COS_FIT):
    turns = turns - ((turns + ROUND) - ROUND)
    square = turns * turns
    sine = turns * horner(sin_fit, square)
    twice = sine + sine
    return twice * horner(cos_fit, square), 1.0 - twice * sine


def sin_cos_fine(turns):
    return sin_cos(turns, SIN_FINE, COS_FINE)


def swap(left, right, shift, low):
    lane = lax.broadcasted_iota(jnp.int32, left.shape, 1)
    moved = jnp.take_along_axis(
        jnp.where(low, right, left), jnp.bitwise_xor(lane, shift), axis=1
    )
    return jnp.where(low, left, moved), jnp.where(low, moved, right)


def in_hbm(value):
    return pltpu.with_memory_space_constraint(value, pltpu.HBM)


def pack_kernel(planes_hbm, out_hbm, in_ref, out_ref, in_sems, out_sems):
    lane = lax.broadcasted_iota(jnp.int32, (8, LANES), 1)
    high = lane >= 2 * LOW
    odd = lane % (2 * LOW) >= LOW
    groups = planes_hbm.shape[1] // 8

    def fetch(g):
        rows = pl.ds(pl.multiple_of(8 * g, 8), 8)
        return pltpu.make_async_copy(planes_hbm.at[:, rows, :], in_ref.at[g], in_sems.at[g])

    def store(g):
        part = pl.ds(pl.multiple_of(g * size, 8), size)
        return pltpu.make_async_copy(out_ref.at[part], out_hbm.at[part], out_sems.at[g])

    def group_step(g, carry):
        fetch(g).wait()
        for m in range(PACKED):
            blocks = [in_ref[g, min(PACK * m + n, PLANES - 1)] for n in range(PACK)]
            blocks = [
                pltpu.roll(block, n * LOW, 1) if n else block for n, block in enumerate(blocks)
            ]
            for r in range(PACK):
                part = [blocks[(k - r) % PACK] for k in range(PACK)]
                turned = jnp.where(
                    high,
                    jnp.where(odd, part[3], part[2]),
                    jnp.where(odd, part[1], part[0]),
                )
                out_ref[pl.ds(g * size + r * PACKED + m, 8, stride=PACK * PACKED), :] = turned
        store(g).start()
        return carry

    size = 8 * PACK * PACKED
    for g in range(groups):
        fetch(g).start()
    lax.fori_loop(0, groups, group_step, 0)
    for g in range(groups):
        store(g).wait()


def pack(planes):
    groups = planes.shape[1] // 8
    return pl.pallas_call(
        pack_kernel,
        in_specs=[pl.BlockSpec(memory_space=pltpu.HBM)],
        out_specs=pl.BlockSpec(memory_space=pltpu.HBM),
        out_shape=pltpu.HBM((DEVICES * PACKED, LANES), jnp.float32),
        scratch_shapes=[
            pltpu.VMEM((groups, PLANES, 8, LANES), jnp.float32),
            pltpu.VMEM((DEVICES * PACKED, LANES), jnp.float32),
            pltpu.SemaphoreType.DMA((groups,)),
            pltpu.SemaphoreType.DMA((groups,)),
        ],
        compiler_params=pltpu.CompilerParams(vmem_limit_bytes=16 * 2**20),
        cost_estimate=pl.CostEstimate(flops=10**6, bytes_accessed=1700000, transcendentals=0),
    )(in_hbm(planes))


def tree_sum(terms):
    while len(terms) > 1:
        terms = [terms[k] + terms[k + 1] for k in range(0, len(terms), 2)]
    return terms[0]


def phase_kernel(
    amp_hbm,
    speed_hbm,
    shift_hbm,
    lane_hbm,
    table_hbm,
    table0_ref,
    first_ref,
    amp_ref,
    speed_ref,
    shift_ref,
    lane_ref,
    table_ref,
    row_ref,
    wave_ref,
    mode_ref,
    mode_smem,
    sems,
    out_sems,
):
    fetches = [
        pltpu.make_async_copy(source, target, sems.at[k])
        for k, (source, target) in enumerate(
            (
                (amp_hbm, amp_ref),
                (speed_hbm, speed_ref),
                (shift_hbm, shift_ref),
                (lane_hbm, lane_ref),
            )
        )
    ]
    for fetch in fetches:
        fetch.start()
    for fetch in fetches:
        fetch.wait()
    device = lax.axis_index(AXES)
    wide_x, wide_y = box_widths(0)
    per_row = TY // LOW
    base_x = (device // per_row).astype(jnp.float32) * wide_x + 0.5 * wide_x
    base_y = (device % per_row).astype(jnp.float32) * (LOW * wide_y) + 0.5 * wide_y

    which = lax.broadcasted_iota(jnp.int32, (MODES, LANES), 0)
    kx = jnp.zeros((MODES, LANES), jnp.float32)
    ky = jnp.zeros((MODES, LANES), jnp.float32)
    for mode in range(MODES):
        kx = jnp.where(which == mode, speed_ref[0, mode], kx)
        ky = jnp.where(which == mode, speed_ref[1, mode], ky)
    for level in range(BITS + 1):
        at = OFFSET_ROW + 2 * level
        turns = kx * lane_ref[at : at + 1, :] + ky * lane_ref[at + 1 : at + 2, :]
        sine, _ = sin_cos_fine(turns)
        half = turns * horner(SIN_FINE, turns * turns)
        at = level * 2 * MODES
        mode_ref[at : at + MODES, :] = -2.0 * half * half
        mode_ref[at + MODES : at + 2 * MODES, :] = sine
    copy = pltpu.make_async_copy(mode_ref, mode_smem, sems.at[4])
    copy.start()

    low = lax.broadcasted_iota(jnp.int32, (LOW, LANES), 0).astype(jnp.float32) * wide_y
    for mode in range(MODES):
        at_base = (
            speed_ref[0, mode] * base_x
            + speed_ref[1, mode] * base_y
            + shift_ref[mode] * (1.0 / TWO_PI)
        )
        sine, cosine = sin_cos_fine(at_base + speed_ref[1, mode] * low)
        row_ref[mode] = amp_ref[mode] * sine
        row_ref[MODES + mode] = amp_ref[mode] * cosine
    copy.wait()

    def differences(source_ref, level, p, groups):
        even = [[] for _ in range(groups)]
        odd = [[] for _ in range(groups)]
        for mode in range(MODES):
            less = mode_smem[level * 2 * MODES + mode, p]
            sine = mode_smem[level * 2 * MODES + MODES + mode, p]
            for t in range(groups):
                rows = slice(8 * t, 8 * t + 8)
                even[t].append(source_ref[mode, rows, :] * less)
                odd[t].append(source_ref[MODES + mode, rows, :] * sine)
        sums = []
        for t in range(groups):
            x, y = tree_sum(even[t]), tree_sum(odd[t])
            sums.append((x + y, x - y))
        return tuple(sums)

    def put(ref, at, rows, turns, scale=None):
        sine, cosine = sin_cos(turns)
        if scale is not None:
            sine, cosine = sine * scale, cosine * scale
        ref[at, rows, :] = cosine
        ref[at + 1, rows, :] = sine

    length = lane_ref[FIRST_ROW : FIRST_ROW + 1, :]

    def first_step(p, carry):
        a = p // CHEB
        b = p - a * CHEB
        line = (
            lane_ref[pl.ds(FIRST_ROW + 1 + a, 1), :]
            + lane_ref[pl.ds(FIRST_ROW + 1 + CHEB + b, 1), :]
        )
        back = (
            lane_ref[pl.ds(FIRST_ROW + CHEB - a, 1), :]
            + lane_ref[pl.ds(FIRST_ROW + 2 * CHEB - b, 1), :]
        )
        for t, (here, there) in enumerate(differences(row_ref, BITS, p, LOW // 8)):
            rows = slice(8 * t, 8 * t + 8)
            put(first_ref, 2 * p, rows, here * length + line)
            put(first_ref, 2 * (NODES - 1 - p), rows, there * length + back)
        return carry

    lax.fori_loop(0, NODES // 2 + 1, first_step, 0)

    def table_copy(level):
        return pltpu.make_async_copy(
            table_ref.at[pl.ds(level * LEVEL_TABLE, LEVEL_TABLE)],
            table_hbm.at[pl.ds((level - 1) * LEVEL_TABLE, LEVEL_TABLE)],
            out_sems.at[level],
        )

    table0_copy = pltpu.make_async_copy(
        table_ref.at[pl.ds(0, LEVEL_TABLE)], table0_ref, out_sems.at[0]
    )

    def level_step(level, carry):
        top = level * TABLE
        apart = [lane_ref[pl.ds(top + c, 1), :] for c in range(2)]
        parent = lane_ref[pl.ds(top + 2, 1), :]
        move_x = lane_ref[pl.ds(top + 3, 1), :]
        move_y = lane_ref[pl.ds(top + 4, 1), :]
        for mode in range(MODES):
            sine, cosine = sin_cos_fine(speed_ref[0, mode] * move_x + speed_ref[1, mode] * move_y)
            old_sine = row_ref[mode, :HALF, :]
            old_cosine = row_ref[MODES + mode, :HALF, :]
            wave_ref[mode] = old_sine * cosine + old_cosine * sine
            wave_ref[MODES + mode] = old_cosine * cosine - old_sine * sine
        moved = [
            (here * parent, there * parent)
            for here, there in differences(wave_ref, level, NODES // 2, HALF // 8)
        ]

        _, child = points_of()

        def row_step(a, inner_carry):
            scale = jnp.float32(1.0)
            for i in range(1, CHEB - 1):
                scale = jnp.where(a == i, float(lagrange_of(child[0, i])[2]), scale)
            lines = [
                (
                    lane_ref[pl.ds(top + 5 + 2 * CHEB * c + a, 1), :],
                    lane_ref[pl.ds(top + 5 + 2 * CHEB * (c + 1) - 1 - a, 1), :],
                )
                for c in range(2)
            ]
            for b in range(CHEB):
                p = a * CHEB + b
                far = differences(wave_ref, level, p, HALF // 8)
                for c in range(2):
                    at = (2 * level + c) * (4 * NODES)
                    for t in range(HALF // 8):
                        rows = slice(8 * t, 8 * t + 8)
                        for k, place in enumerate((2 * p, 2 * (2 * NODES - 1 - p))):
                            turns = far[t][k] * apart[c] + (moved[t][k] + lines[c][k])
                            put(table_ref, at + place, rows, turns, scale)
            return inner_carry

        lax.fori_loop(0, CHEB, row_step, 0)
        return carry

    def later_step(level, carry):
        level_step(level, carry)
        table_copy(level).start()
        return carry

    level_step(0, 0)
    table0_copy.start()
    lax.fori_loop(1, BITS, later_step, 0)
    table0_copy.wait()
    for level in range(1, BITS):
        table_copy(level).wait()


def phases(speed_amp, speed_wave, speed_shift, lanes):
    return pl.pallas_call(
        phase_kernel,
        in_specs=[pl.BlockSpec(memory_space=pltpu.HBM)] * 4,
        out_specs=[
            pl.BlockSpec(memory_space=pltpu.HBM),
            pl.BlockSpec(memory_space=pltpu.VMEM),
            pl.BlockSpec(memory_space=pltpu.VMEM),
        ],
        out_shape=[
            pltpu.HBM(((BITS - 1) * LEVEL_TABLE, HALF, LANES), jnp.float32),
            pltpu.VMEM((LEVEL_TABLE, HALF, LANES), jnp.float32),
            pltpu.VMEM((2 * NODES, LOW, LANES), jnp.float32),
        ],
        scratch_shapes=[
            pltpu.SMEM((MODES,), jnp.float32),
            pltpu.SMEM((2, MODES), jnp.float32),
            pltpu.SMEM((MODES,), jnp.float32),
            pltpu.VMEM(lanes.shape, jnp.float32),
            pltpu.VMEM((BITS * LEVEL_TABLE, HALF, LANES), jnp.float32),
            pltpu.VMEM((2 * MODES, LOW, LANES), jnp.float32),
            pltpu.VMEM((2 * MODES, HALF, LANES), jnp.float32),
            pltpu.VMEM(((BITS + 1) * 2 * MODES, LANES), jnp.float32),
            pltpu.SMEM(((BITS + 1) * 2 * MODES, LANES), jnp.float32),
            pltpu.SemaphoreType.DMA((6,)),
            pltpu.SemaphoreType.DMA((BITS,)),
        ],
        compiler_params=pltpu.CompilerParams(vmem_limit_bytes=32 * 2**20),
        cost_estimate=pl.CostEstimate(
            flops=70 * 10**6, bytes_accessed=13 * 10**6, transcendentals=3 * 10**6
        ),
    )(*map(in_hbm, (speed_amp, speed_wave, speed_shift, lanes)))


def level_kernel(
    got_ref,
    table_hbm,
    table0_ref,
    first_ref,
    out_hbm,
    state_ref,
    other_ref,
    table_ref,
    out_ref,
    slot0_ref,
    slot1_ref,
    sems,
    out_sems,
):
    copies = []
    for level in range(BITS - 1):
        part = pl.ds(level * LEVEL_TABLE, LEVEL_TABLE)
        copies.append(
            pltpu.make_async_copy(table_hbm.at[part], table_ref.at[part], sems.at[level])
        )
    for copy in copies:
        copy.start()
    turn = lax.axis_index(AXES) % PACK

    def unpack(m):
        block = got_ref[pl.ds(m, DEVICES, stride=PACKED), :].T
        for n in range(PACK):
            plane = PACK * m + lax.rem(n + PACK - turn, PACK)
            state_ref[pl.ds(pl.multiple_of(plane * LOW, LOW), LOW), :] = block[
                n * LOW : (n + 1) * LOW, :
            ]

    def unpack_step(k, carry):
        for m in range(3):
            unpack(3 * k + m)
        return carry

    unpack(PACKED - 1)
    lax.fori_loop(0, PACKED // 3, unpack_step, 0)
    lane = lax.broadcasted_iota(jnp.int32, (8, LANES), 1)
    order = lane % 2
    for bit in range(1, BITS):
        order = order + ((lane >> (BITS - bit)) % 2 << bit)

    def places_of(level, b):
        return [a * CHEB + b if split_first(level) else b * CHEB + a for a in range(CHEB)]

    slots = (slot0_ref, slot1_ref)
    states = (state_ref, other_ref)

    def fetch(level, b, t):
        shift = 2 ** LANE_BIT[level]
        low = lane // shift % 2 == 0
        for a, at in enumerate(places_of(level, b)):
            pair = []
            for half in range(2):
                row = half * HALF + 8 * t
                re = states[level % 2][pl.ds(at * LOW + row, 8), :]
                im = states[level % 2][pl.ds((NODES + at) * LOW + row, 8), :]
                if level == 0:
                    rows = slice(row, row + 8)
                    cosine, sine = first_ref[2 * at, rows, :], first_ref[2 * at + 1, rows, :]
                    re, im = re * cosine - im * sine, re * sine + im * cosine
                pair.append((re, im))
            for r in range(2):
                for c, value in enumerate(swap(pair[0][r], pair[1][r], shift, low)):
                    slots[t][(2 * a + r) * 2 + c] = value

    def split(level, b, t, values):
        rows = slice(8 * t, 8 * t + 8)
        places = places_of(level, b)

        def rotated(half, a, near):
            real = imag = None
            for c in range(2):
                table = table_ref if level else table0_ref
                e = 2 * ((2 * c + half) * NODES + a * CHEB + b)
                e = e + max(level - 1, 0) * LEVEL_TABLE
                cosine, sine = table[e, rows, :], table[e + 1, rows, :]
                re, im = near[0][c], near[1][c]
                new_re, new_im = re * cosine - im * sine, re * sine + im * cosine
                real = new_re if c == 0 else real + new_re
                imag = new_im if c == 0 else imag + new_im
            return real, imag

        def keep(a, totals):
            for r in range(2):
                first, second = totals[0][r], totals[1][r]
                if level == BITS - 1:
                    first, second = swap(first, second, 1, lane % 2 == 0)
                    for half, value in enumerate((first, second)):
                        at_row = (half * HALF + 8 * t) * 2 + r
                        out_ref[a, b, pl.ds(at_row, 8, stride=2), :] = jnp.take_along_axis(
                            value, order, axis=1
                        )
                    continue
                at_row = (r * NODES + places[a]) * LOW + 8 * t
                states[1 - level % 2][pl.ds(at_row, 8), :] = first
                states[1 - level % 2][pl.ds(at_row + HALF, 8), :] = second

        ends = [[[values[a][r][c] for c in range(2)] for r in range(2)] for a in (0, 2, 4)]
        keep(0, (rotated(0, 0, ends[1]), rotated(1, 0, ends[0])))
        keep(4, (rotated(0, 4, ends[2]), rotated(1, 4, ends[1])))
        parts = [
            [
                (
                    values[0][r][c] + values[4][r][c],
                    values[1][r][c] + values[3][r][c],
                    values[0][r][c] - values[4][r][c],
                    values[1][r][c] - values[3][r][c],
                    values[2][r][c],
                )
                for c in range(2)
            ]
            for r in range(2)
        ]
        _, child = points_of()
        held = {}
        for i in range(1, CHEB - 1):
            row = lagrange_of(child[0, i])
            row = row / row[2]
            sums, gaps = [[], []], [[], []]
            for r in range(2):
                for c in range(2):
                    even0, even1, odd0, odd1, middle = parts[r][c]
                    even = (
                        float((row[0] + row[4]) / 2) * even0
                        + float((row[1] + row[3]) / 2) * even1
                        + middle
                    )
                    odd = (
                        float((row[0] - row[4]) / 2) * odd0
                        + float((row[1] - row[3]) / 2) * odd1
                    )
                    sums[r].append(even + odd)
                    gaps[r].append(even - odd)
            held[0, i] = rotated(0, i, sums)
            held[1, CHEB - 1 - i] = rotated(1, CHEB - 1 - i, gaps)
            for a in range(1, CHEB - 1):
                if (0, a) in held and (1, a) in held:
                    keep(a, (held.pop((0, a)), held.pop((1, a))))

    def out_copy(b):
        return pltpu.make_async_copy(out_ref.at[:, b], out_hbm.at[:, b], out_sems.at[b])

    for level in range(BITS):
        if level:
            copies[level - 1].wait()
        for t in range(HALF // 8):
            fetch(level, 0, t)

        def step(b, carry, level=level):
            for t in range(HALF // 8):
                values = [
                    [[slots[t][(2 * a + r) * 2 + c] for c in range(2)] for r in range(2)]
                    for a in range(CHEB)
                ]
                fetch(level, jnp.minimum(b + 1, CHEB - 1), t)
                split(level, b, t, values)
            if level == BITS - 1:
                out_copy(b).start()
            return carry

        lax.fori_loop(0, CHEB, step, 0)
    for b in range(CHEB):
        out_copy(b).wait()


def levels(got, table, table0, first):
    return pl.pallas_call(
        level_kernel,
        in_specs=[
            pl.BlockSpec(memory_space=pltpu.VMEM),
            pl.BlockSpec(memory_space=pltpu.HBM),
            pl.BlockSpec(memory_space=pltpu.VMEM),
            pl.BlockSpec(memory_space=pltpu.VMEM),
        ],
        out_specs=pl.BlockSpec(memory_space=pltpu.HBM),
        out_shape=pltpu.HBM((CHEB, CHEB, 2 * LOW, LANES), jnp.float32),
        scratch_shapes=[
            pltpu.VMEM((PACK * PACKED * LOW, LANES), jnp.float32),
            pltpu.VMEM((PLANES * LOW, LANES), jnp.float32),
            pltpu.VMEM(((BITS - 1) * LEVEL_TABLE, HALF, LANES), jnp.float32),
            pltpu.VMEM((CHEB, CHEB, 2 * LOW, LANES), jnp.float32),
            pltpu.VMEM((4 * CHEB, 8, LANES), jnp.float32),
            pltpu.VMEM((4 * CHEB, 8, LANES), jnp.float32),
            pltpu.SemaphoreType.DMA((BITS - 1,)),
            pltpu.SemaphoreType.DMA((CHEB,)),
        ],
        compiler_params=pltpu.CompilerParams(vmem_limit_bytes=32 * 2**20),
        cost_estimate=pl.CostEstimate(
            flops=22 * 10**6, bytes_accessed=14 * 10**6, transcendentals=0
        ),
    )(got, in_hbm(table), table0, first)


def on_device(coefficients, speed_amp, speed_wave, speed_shift):
    packed = pack(coefficients.reshape(PLANES, DEVICES // PACK, LANES))
    sent = packed.reshape(DEVICES, 1, PACKED * LANES)
    got = lax.all_to_all(sent, AXES, 0, 0, tiled=True)
    got = got.reshape(DEVICES * PACKED, LANES)
    table, table0, first = phases(speed_amp, speed_wave, speed_shift, jnp.asarray(lane_tables()))
    final = levels(got, table, table0, first).reshape(CHEB, CHEB, LOW, 2, LANES)
    return final.transpose(3, 0, 1, 2, 4).reshape(2, CHEB, CHEB, LOW * LANES)


def solution(mesh):
    in_specs = (P(None, None, None, AXES, None), P(), P(), P())
    out_specs = P(None, None, None, AXES)
    return jax.shard_map(
        on_device, mesh=mesh, in_specs=in_specs, out_specs=out_specs, check_vma=False
    )
```
